32 devices in a mesh: phase: 4 (over z), vox: 8 (over y, x, core).
Axes of the slice: x: 2, y: 2, z: 4, core: 2. Of those that a mesh axis runs over, the one named last changes fastest.
Arguments:
- influence: float32 [4, 16384, 1536], P('phase', 'vox'), may hold values from -0.15625 to 0.15625
- weights: float32 [1536, 128], P(('phase', 'vox')), may hold values from 0.5 to 2
- warp_tiles: float32 [64, 128, 128], replicated, may hold values from -0.5 to 0.5
- owners: int32 [4, 128, 1], P('phase', 'vox'), may hold values from 0 to 7; in each aligned block of 16 rows (0 to 15, 16 to 31, ..., all dimensions but the last counted through in order) at most 2 rows name the same one
- owner_slot: int32 [4, 128], P('phase', 'vox'), may hold values from 0 to 15
- tile_index: int32 [4, 128], P('phase', 'vox'), may hold values from 0 to 63
- structure: int32 [16384], P('vox'), may hold values from 0 to 7
- prescribed: float32 [8, 128], replicated, may hold values from 0 to 3
- importance: float32 [8], replicated, may hold values from 0.25 to 4
- step_size: float32 [128], replicated, may hold values from 0.02 to 0.08
Outputs:
- new_weights: float32 [1536, 128], P(('phase', 'vox'))
- dose_field: float32 [16384, 128], P('vox')
The draws below stay inside these ranges and needn't reach their ends.
Inputs may be any that keep to these rules, and one draw needn't show every extreme that they name: `owners`: for each phase and each device of vox, at most 2 of that device's 16 blocks name one owner, and some device reaches 2.
All inputs are finite; a program needn't handle non-finite values.
Results may differ from the reference program's by a relative error of at most 0.00023.
Values sent between devices are 32-bit elements; how exact they have to be, the bound alone decides.
No kernel may reach another device: no remote copies, remote signals or barrier semaphores. Data moves between devices by JAX's collectives and lax.ppermute only.
A program may use at most 128 MiB of HBM per device.

```python
import math
import jax
import jax.numpy as jnp
import numpy as np
from jax import lax

SPOTS = 1536
PLANS = 128
BLK = 128
CAP = 2
NTILE = 64
NSTRUCT = 8
ITERS = 2
PHASES = 4
VOXELS = 16384
BLK_DEV = 16
NBLK = 128
N_VOX = 8


def plant(entries, stream_key, least, high):
    longest = entries.shape.index(max(entries.shape))
    spots = []
    for shift in (0, 1):
        where = [jax.random.randint(jax.random.fold_in(stream_key, axis), (), 0, length) for axis, length in enumerate(entries.shape)]
        where[longest] = (where[longest] + shift) % entries.shape[longest]
        spots.append(tuple(where))
    return entries.at[spots[0]].set(least).at[spots[1]].set(high)


def shard_levels(own_key, dims, split, smallest, top_value):
    factor_of = 1.0
    for position, parts in split:
        heights = jax.random.uniform(jax.random.fold_in(jax.random.fold_in(own_key, 6), position), (parts,), jnp.float32, smallest / len(split), top_value / len(split))
        factor_of = factor_of * jnp.repeat(jnp.exp(heights), dims[position] // parts).reshape((-1,) + (1,) * (len(dims) - 1 - position))
    return factor_of


def deal_out(rng, own, number, rows, number_of, top, bound, skew):
    sequence = jax.random.permutation(rng, number_of)
    heavy_load, ordinary = load_shares(number_of, rows * top, bound, skew, True), load_shares(number_of, rows * top, bound, skew, False)
    places = jnp.arange(number_of)

    def named(lengths, offset_by):
        used = int((lengths > 0).sum())
        fixed = max(1, used // 4)
        passed = fixed + (places - fixed + offset_by * (used - fixed)) % max(1, number_of - fixed)
        return jnp.zeros((number_of,), jnp.int32).at[sequence[jnp.where(places < fixed, places, passed)]].set(jnp.asarray(lengths, jnp.int32))

    lengths = jnp.where(number % 4 == 0, named(heavy_load, number // 4), named(ordinary, number - number // 4 - 1))
    mixed = jax.random.permutation(jax.random.fold_in(own, 3), number_of)
    giver, sink = mixed[0:number_of // 2 * 2:2], mixed[1:number_of // 2 * 2:2]
    room = jnp.minimum(lengths[giver] - 1, bound - lengths[sink]) // 2
    room = jnp.where((giver == sequence[0]) | (sink == sequence[0]) | (lengths[sink] == 0), 0, jnp.maximum(room, 0))
    passed = jax.random.randint(jax.random.fold_in(own, 4), (number_of // 2,), 0, 1 << 20) % (room + 1)
    lengths = lengths.at[giver].add(-passed).at[sink].add(passed)
    labels = jnp.searchsorted(jnp.cumsum(lengths), jnp.arange(rows * top), side="right").astype(jnp.int32)
    grid = labels.reshape(top, rows).T
    grid = grid[jax.random.permutation(jax.random.fold_in(own, 1), rows)]
    offset_by = jax.random.randint(jax.random.fold_in(own, 2), (rows, 1), 0, top)
    return jnp.take_along_axis(grid, (jnp.arange(top)[None, :] + offset_by) % top, axis=1)


def load_shares(number_of, total, limit, lean, full):
    portions = [(1 << 20) // math.isqrt(rank ** lean) + 1 for rank in range(1, number_of + 1)]
    largest = limit if full else min(limit, max(-(-total // number_of), total * portions[0] // sum(portions)))
    least = 1 if total - largest >= number_of - 1 else 0
    given, surplus = [largest] + [least] * (number_of - 1), total - largest - least * (number_of - 1)
    while surplus > 0:
        movable = [i for i in range(1, number_of) if given[i] < largest] or [i for i in range(1, number_of) if given[i] < limit]
        mass, budget = sum([portions[i] for i in movable]), surplus
        for i in movable:
            addition = min(limit - given[i], max(1, budget * portions[i] // mass), surplus)
            given[i] = given[i] + addition
            surplus = surplus - addition
    return np.array(given)


def gaussian(key, extent, deviation, bound, cuts=(), kind=jnp.bfloat16):
    values = jax.random.normal(key, extent, jnp.float32) * deviation
    if len(cuts) > 0:
        values = shard_levels(key, extent, cuts, -0.22, 0.18) * values
    return jnp.clip(values, min=-bound, max=bound).astype(kind)


def setup_inputs(seed: int = 0) -> dict:
    keys = jax.random.split(jax.random.key(seed), 11)
    influence = gaussian(keys[0], (PHASES, VOXELS, SPOTS), SPOTS ** -0.5, 0.15625, ((0, 4), (1, 8)), jnp.float32)
    weights = jnp.clip(jnp.exp(math.log(2.0) - 1.3862944 * jax.random.uniform(keys[1], (SPOTS, PLANS), jnp.float32) ** shard_levels(keys[1], (SPOTS, PLANS), ((0, 32),), -0.2, 0.2)), 0.5, 2.0)
    warp_tiles = gaussian(keys[2], (NTILE, BLK, BLK), BLK ** -0.5, 0.5, (), jnp.float32)
    owners_keys = jax.random.split(jax.random.fold_in(keys[3], 1), PHASES * NBLK // BLK_DEV)
    owners_turns = jax.random.permutation(jax.random.fold_in(keys[3], 3), PHASES * NBLK // BLK_DEV)
    owners = jax.vmap(lambda own, number: deal_out(jax.random.fold_in(keys[3], 2), own, number, BLK_DEV, N_VOX, 1, CAP, 2))(owners_keys, owners_turns).reshape((PHASES, NBLK, 1))
    owner_slot = plant(jax.random.randint(keys[4], (PHASES, NBLK), 0, BLK_DEV), jax.random.fold_in(keys[4], 1), 0, BLK_DEV - 1).astype(jnp.int32)
    tile_index = plant(jax.random.randint(keys[5], (PHASES, NBLK), 0, NTILE), jax.random.fold_in(keys[5], 1), 0, NTILE - 1).astype(jnp.int32)
    structure = plant(jax.random.randint(keys[6], (VOXELS,), 0, NSTRUCT), jax.random.fold_in(keys[6], 1), 0, NSTRUCT - 1).astype(jnp.int32)
    prescribed = jnp.clip(jax.random.uniform(keys[7], (NSTRUCT, PLANS), jnp.float32, 0.0, 3.0), 0.0, 3.0)
    importance = jnp.clip(jnp.exp(jax.random.uniform(keys[8], (NSTRUCT,), jnp.float32, math.log(0.25), math.log(4.0))), 0.25, 4.0)
    step_size = jnp.clip(jnp.exp(jax.random.uniform(keys[9], (PLANS,), jnp.float32, math.log(0.02), math.log(0.08))), 0.02, 0.08)
    return dict(influence=influence, weights=weights, warp_tiles=warp_tiles, owners=owners, owner_slot=owner_slot, tile_index=tile_index, structure=structure, prescribed=prescribed, importance=importance, step_size=step_size)


def reference(influence, weights, warp_tiles, owners, owner_slot, tile_index, structure, prescribed, importance, step_size):
    highest = lax.Precision.HIGHEST
    num_blocks = VOXELS // BLK
    member = (structure[:, None] == jnp.arange(NSTRUCT, dtype=jnp.int32)[None, :]).astype(jnp.float32)
    target_dose = jnp.dot(member, prescribed, precision=highest, preferred_element_type=jnp.float32)
    voxel_weight = jnp.dot(member, importance[:, None], precision=highest, preferred_element_type=jnp.float32)
    new_weights = weights
    dose_field = jnp.zeros((VOXELS, PLANS), jnp.float32)
    for iteration in range(ITERS):
        summed = jnp.zeros((num_blocks, BLK, PLANS), jnp.float32)
        for phase_index in range(PHASES):
            phase_dose = jnp.dot(influence[phase_index], new_weights, precision=highest, preferred_element_type=jnp.float32)
            blocks = phase_dose.reshape(num_blocks, BLK, PLANS)
            chosen = warp_tiles[tile_index[phase_index]]
            warped = jnp.einsum("kab,kbp->kap", chosen, blocks, precision=highest)
            target = (owners[phase_index, :, 0] * BLK_DEV + owner_slot[phase_index]).astype(jnp.int32)
            summed = summed + jax.ops.segment_sum(warped, target, num_segments=num_blocks)
        dose_field = summed.reshape(VOXELS, PLANS)
        adjoint = voxel_weight * (dose_field - target_dose)
        adjoint_blocks = adjoint.reshape(num_blocks, BLK, PLANS)
        gradient = jnp.zeros((SPOTS, PLANS), jnp.float32)
        for phase_index in range(PHASES):
            chosen = warp_tiles[tile_index[phase_index]]
            target = (owners[phase_index, :, 0] * BLK_DEV + owner_slot[phase_index]).astype(jnp.int32)
            pulled = adjoint_blocks[target]
            local_adjoint = jnp.einsum("kab,kap->kbp", chosen, pulled, precision=highest).reshape(VOXELS, PLANS)
            gradient = gradient + jnp.dot(influence[phase_index].T, local_adjoint, precision=highest, preferred_element_type=jnp.float32)
        new_weights = jnp.maximum(new_weights - step_size[None, :] * gradient, 0.0)
    return new_weights, dose_field
```

```python
import jax
import jax.numpy as jnp
from jax import lax
from jax.sharding import PartitionSpec as P

CAP = 2
NSTRUCT = 8
ITERS = 2
VOX = "vox"
PHASE = "phase"
LABEL_ROWS = 8


def swap(x, axis, mask):
    count = lax.axis_size(axis)
    return lax.ppermute(x, axis, [(i, i ^ mask) for i in range(count)])


def spread(x, axis, masks):
    return [x] + [swap(x, axis, m) for m in masks]


def core_count():
    return min(2, lax.axis_size(VOX))


def gather_weights(shard, extra):
    phases, vox = lax.axis_size(PHASE), lax.axis_size(VOX)
    by_phase = jnp.concatenate(spread(shard, PHASE, range(1, phases)), axis=0)
    if extra is not None:
        by_phase = jnp.concatenate([by_phase, extra], axis=0)
    cores = core_count()
    by_chip = jnp.stack(spread(by_phase, VOX, range(cores, vox, cores)))
    both = jnp.stack(spread(by_chip, VOX, range(1, cores)), axis=1)
    both = both.reshape(vox, by_phase.shape[0], shard.shape[1])
    rows = phases * shard.shape[0]
    return both[:, :rows].reshape(vox, phases, *shard.shape), both[:, rows:]


def scatter_sum(parts):
    vox, phases = parts.shape[:2]
    cores = core_count()
    split = parts.reshape(vox // cores, cores, phases, *parts.shape[2:])
    chips = split[:, 0]
    for m in range(1, cores):
        chips = chips + swap(split[:, m], VOX, m)
    mine = chips[0]
    for m in range(1, vox // cores):
        mine = mine + swap(chips[m], VOX, m * cores)
    total = mine[0]
    for m in range(1, phases):
        total = total + swap(mine[m], PHASE, m)
    return total


def phase_sum(x):
    phases = lax.axis_size(PHASE)
    if phases == 1:
        return x
    z = lax.axis_index(PHASE)
    which = (z ^ (z >> 1)) & 1
    half = x.shape[0] // 2
    keep = lax.dynamic_slice_in_dim(x, which * half, half)
    give = lax.dynamic_slice_in_dim(x, (1 - which) * half, half)
    keep = keep + swap(give, PHASE, 1)
    span = 4
    while span <= phases:
        keep = keep + swap(keep, PHASE, span - 1)
        span *= 2
    other = swap(keep, PHASE, 1)
    low = jnp.where(which == 0, keep, other)
    high = jnp.where(which == 0, other, keep)
    return jnp.concatenate([low, high], axis=0)


def exchange(x):
    return jnp.stack([x[0]] + [swap(x[m], VOX, m) for m in range(1, x.shape[0])])


def per_device(
    influence,
    weights,
    warp_tiles,
    owners,
    owner_slot,
    tile_index,
    structure,
    prescribed,
    importance,
    step_size,
):
    highest = lax.Precision.HIGHEST
    high = lax.Precision.HIGH
    matrix = influence[0]
    vox_rows, spots = matrix.shape
    block_rows = warp_tiles.shape[1]
    plans = weights.shape[1]
    local_blocks = vox_rows // block_rows
    vox_count = lax.axis_size(VOX)
    phases = lax.axis_size(PHASE)
    me_vox = lax.axis_index(VOX)
    me_phase = lax.axis_index(PHASE)
    slots_all = vox_count * CAP
    targets = owners[0, :, 0]
    my_slots = owner_slot[0]
    my_tiles = tile_index[0]

    def orders(names):
        before = jnp.tril(jnp.ones((local_blocks, local_blocks), jnp.int32), -1)
        same = (names[..., :, None] == names[..., None, :]).astype(jnp.int32)
        return jnp.sum(same * before, axis=-1)

    position = (targets ^ me_vox) * CAP + orders(targets)
    chosen_mask = jnp.arange(slots_all, dtype=jnp.int32)[:, None] == position[None, :]
    source = jnp.sum(
        jnp.where(chosen_mask, jnp.arange(1, local_blocks + 1, dtype=jnp.int32)[None, :], 0), axis=1
    )
    labels = jnp.zeros((LABEL_ROWS, plans), jnp.float32)
    labels = labels.at[0, :local_blocks].set(targets.astype(jnp.float32))
    labels = labels.at[1, :local_blocks].set(my_slots.astype(jnp.float32))

    own_tiles = warp_tiles[my_tiles]
    member = (structure[:, None] == jnp.arange(NSTRUCT, dtype=jnp.int32)[None, :]).astype(
        jnp.float32
    )
    target_dose = jnp.dot(member, prescribed, precision=highest, preferred_element_type=jnp.float32)
    voxel_weight = jnp.dot(
        member, importance[:, None], precision=highest, preferred_element_type=jnp.float32
    )
    place_vox = jnp.arange(vox_count) ^ me_vox
    place_phase = jnp.arange(phases) ^ me_phase

    new_weights = weights
    dose_field = jnp.zeros((vox_rows, plans), jnp.float32)
    for iteration in range(ITERS):
        pieces, infos = gather_weights(new_weights, labels if iteration == 0 else None)
        if iteration == 0:
            names = infos[:, 0, :local_blocks].astype(jnp.int32)
            slots = infos[:, 1, :local_blocks].astype(jnp.int32)
            order = jnp.where(names == me_vox, orders(names), -1)
            hit = order[:, None, :] == jnp.arange(CAP, dtype=jnp.int32)[None, :, None]
            received = jnp.sum(jnp.where(hit, slots[:, None, :] + 1, 0), axis=-1).reshape(slots_all) - 1
        whole = pieces[place_vox][:, place_phase]
        whole = whole.transpose(1, 0, 2, 3).reshape(spots, plans)
        phase_dose = jnp.dot(matrix, whole, precision=high, preferred_element_type=jnp.float32)
        blocks = phase_dose.reshape(local_blocks, block_rows, plans)
        warped = jnp.einsum("kab,kbp->kap", own_tiles, blocks, precision=high)
        padded = jnp.concatenate([jnp.zeros_like(warped[:1]), warped], axis=0)
        outgoing = padded[source].reshape(vox_count, CAP, block_rows, plans)
        incoming = exchange(outgoing).reshape(slots_all, block_rows, plans)
        partial_dose = (
            jnp.zeros((local_blocks + 1, block_rows, plans), jnp.float32).at[received].add(incoming)
        )[:local_blocks]
        field = phase_sum(partial_dose)
        dose_field = field.reshape(vox_rows, plans)
        adjoint = (voxel_weight * (dose_field - target_dose)).reshape(local_blocks, block_rows, plans)
        back = adjoint[jnp.maximum(received, 0)].reshape(vox_count, CAP, block_rows, plans)
        returned = exchange(back).reshape(slots_all, block_rows, plans)
        pulled = returned[position]
        local_adjoint = jnp.einsum("kab,kap->kbp", own_tiles, pulled, precision=high)
        gradient = lax.dot_general(
            matrix,
            local_adjoint.reshape(vox_rows, plans),
            (((0,), (0,)), ((), ())),
            precision=high,
            preferred_element_type=jnp.float32,
        )
        parts = gradient.reshape(phases, vox_count, spots // (phases * vox_count), plans)
        parts = parts[place_phase][:, place_vox].transpose(1, 0, 2, 3)
        total = scatter_sum(parts)
        new_weights = jnp.maximum(new_weights - step_size[None, :] * total, 0.0)
    return (new_weights, dose_field)


def solution(mesh):
    in_specs = (
        P("phase", "vox", None),
        P(("phase", "vox"), None),
        P(),
        P("phase", "vox", None),
        P("phase", "vox"),
        P("phase", "vox"),
        P("vox"),
        P(),
        P(),
        P(),
    )
    out_specs = (P(("phase", "vox"), None), P("vox", None))
    return jax.shard_map(
        per_device, mesh=mesh, in_specs=in_specs, out_specs=out_specs, check_vma=False
    )
```

```python
import functools

import jax
import jax.numpy as jnp
from jax import lax
from jax.experimental import pallas as pl
from jax.experimental.pallas import tpu as pltpu
from jax.sharding import PartitionSpec as P

CAP = 2
NSTRUCT = 8
ITERS = 2
CHUNKS = 2
VOX = "vox"
PHASE = "phase"
LABEL_ROWS = 16
F32 = jnp.float32
BF16 = jnp.bfloat16
LARGE = 28 << 20
SMALL = 8 << 20


def swap(x, axis, mask):
    count = lax.axis_size(axis)
    return lax.ppermute(x, axis, [(i, i ^ mask) for i in range(count)])


def spread(x, axis, masks):
    return [x] + [swap(x, axis, m) for m in masks]


def core_count():
    return min(2, lax.axis_size(VOX))


def halves(x, axis):
    big = x.astype(BF16)
    small = (x - big.astype(F32)).astype(BF16)
    return jnp.concatenate([big, small], axis=axis)


def product(left, right):
    rows, cols = left.shape[0], right.shape[1]
    full = jnp.dot(halves(left, 0), halves(right, 1), preferred_element_type=F32)
    return full[:rows, :cols] + (full[:rows, cols:] + full[rows:, :cols])


def split_pieces(me_ref, out, pieces, rows, vox, phases):
    cores = len(pieces)
    for c, ref in enumerate(pieces):
        for k in range(vox // cores):
            for p in range(phases):
                v = me_ref[0] ^ (k * cores + c)
                at = ((me_ref[1] ^ p) * vox + v) * rows
                out[pl.ds(pl.multiple_of(at, rows), rows), :] = halves(
                    ref[k, p * rows : (p + 1) * rows, :], 1
                )


def forward_body(
    dims, source_ref, valid_ref, tile_ref, me_ref, *refs
):
    vox, phases, rows, pieces_n, chunks = dims
    blocks, tiles = refs[:CAP], refs[CAP : 2 * CAP]
    pieces = refs[2 * CAP : 2 * CAP + pieces_n]
    outs = refs[2 * CAP + pieces_n : -1]
    terms = refs[-1]
    step = pl.program_id(0)
    height = blocks[0].shape[0]
    plans = terms.shape[1] // 2

    @pl.when(step == 0)
    def _():
        if len(pieces[0].shape) == 2:
            terms[...] = halves(pieces[0][...], 1)
        else:
            split_pieces(me_ref, terms, pieces, rows, vox, phases)

    rows_now = jnp.concatenate([b[...] for b in blocks], axis=0)
    full = jnp.dot(halves(rows_now, 0), terms[...], preferred_element_type=F32)
    n = rows_now.shape[0]
    dose = full[:n, :plans] + (full[:n, plans:] + full[n:, :plans])
    part = height // chunks
    for j in range(CAP):
        warped = product(tiles[j][0], dose[j * height : (j + 1) * height])
        warped = jnp.where(valid_ref[step * CAP + j] > 0, warped, 0.0)
        for m in range(vox):

            @pl.when(step == m)
            def _():
                for h in range(chunks):
                    outs[h * vox + m][j] = warped[h * part : (h + 1) * part]


def block_specs(height, spots, tile_shape):
    specs = []
    for j in range(CAP):
        specs.append(
            pl.BlockSpec((height, spots), lambda m, s, v, t, e, j=j: (s[m * CAP + j], 0))
        )
    for j in range(CAP):
        specs.append(
            pl.BlockSpec((1, *tile_shape), lambda m, s, v, t, e, j=j: (t[m * CAP + j], 0, 0))
        )
    return specs


def whole(shape):
    return pl.BlockSpec(shape, lambda *_: (0,) * len(shape))


def forward(scalars, matrix, warp_tiles, pieces, rows, vox, phases):
    height = warp_tiles.shape[1]
    spots = matrix.shape[1]
    plans = pieces[0].shape[-1]
    out = jax.ShapeDtypeStruct((CAP, height // CHUNKS, plans), F32)
    flops = 2 * matrix.size * plans * 4
    return pl.pallas_call(
        functools.partial(forward_body, (vox, phases, rows, len(pieces), CHUNKS)),
        grid_spec=pltpu.PrefetchScalarGridSpec(
            num_scalar_prefetch=4,
            grid=(vox,),
            in_specs=block_specs(height, spots, warp_tiles.shape[1:])
            + [whole(p.shape) for p in pieces],
            out_specs=[whole(out.shape)] * (vox * CHUNKS),
            scratch_shapes=[pltpu.VMEM((spots, 2 * plans), BF16)],
        ),
        out_shape=[out] * (vox * CHUNKS),
        compiler_params=pltpu.CompilerParams(
            vmem_limit_bytes=LARGE, dimension_semantics=("arbitrary",)
        ),
        cost_estimate=pl.CostEstimate(
            flops=flops, bytes_accessed=matrix.size * 4, transcendentals=0
        ),
        name="dose_and_warp",
    )(*scalars, *([matrix] * CAP), *([warp_tiles] * CAP), *pieces)


def gradient_body(dims, source_ref, valid_ref, tile_ref, me_ref, *refs):
    vox, phases, rows, cores, chunks = dims
    blocks, tiles = refs[:CAP], refs[CAP : 2 * CAP]
    returned = refs[2 * CAP : 2 * CAP + vox * chunks]
    outs = refs[2 * CAP + vox * chunks : -3]
    adjoint, total, turned = refs[-3:]
    step = pl.program_id(0)
    plans = adjoint.shape[-1]
    part = adjoint.shape[1] // chunks

    @pl.when(step == 0)
    def _():
        total[...] = jnp.zeros_like(total)

    for m in range(vox):

        @pl.when(step == m)
        def _():
            for h in range(chunks):
                adjoint[:, h * part : (h + 1) * part, :] = returned[h * vox + m][...]

    columns = []
    for j in range(CAP):
        pulled = product(adjoint[j].T, tiles[j][0])
        columns.append(jnp.where(valid_ref[step * CAP + j] > 0, pulled, 0.0))
    left = halves(jnp.concatenate(columns, axis=1), 0)
    rows_now = jnp.concatenate([b[...] for b in blocks], axis=0)
    big = rows_now.astype(BF16)
    small = (rows_now - big.astype(F32)).astype(BF16)
    first = jnp.dot(left, big, preferred_element_type=F32)
    second = jnp.dot(left[:plans], small, preferred_element_type=F32)
    total[...] += first[:plans] + (first[plans:] + second)

    @pl.when(step == vox - 1)
    def _():
        spots = total.shape[1]
        if len(outs[0].shape) == 2:
            for i in range(spots // plans):
                outs[0][i * plans : (i + 1) * plans, :] = total[:, i * plans : (i + 1) * plans].T
        else:
            for i in range(spots // plans):
                turned[i * plans : (i + 1) * plans, :] = total[:, i * plans : (i + 1) * plans].T
            for c in range(cores):
                for k in range(vox // cores):
                    for p in range(phases):
                        v = me_ref[0] ^ (k * cores + c)
                        at = ((me_ref[1] ^ p) * vox + v) * rows
                        outs[c][k, p] = turned[pl.ds(pl.multiple_of(at, rows), rows), :]


def gradient_parts(scalars, matrix, warp_tiles, returned, rows, vox, phases):
    height = warp_tiles.shape[1]
    spots = matrix.shape[1]
    plans = returned[0].shape[-1]
    cores = core_count()
    if rows % 8 == 0:
        outs = [jax.ShapeDtypeStruct((vox // cores, phases, rows, plans), F32)] * cores
    else:
        outs = [jax.ShapeDtypeStruct((spots, plans), F32)]
    return pl.pallas_call(
        functools.partial(gradient_body, (vox, phases, rows, cores, CHUNKS)),
        grid_spec=pltpu.PrefetchScalarGridSpec(
            num_scalar_prefetch=4,
            grid=(vox,),
            in_specs=block_specs(height, spots, warp_tiles.shape[1:])
            + [whole(p.shape) for p in returned],
            out_specs=[whole(o.shape) for o in outs],
            scratch_shapes=[
                pltpu.VMEM((CAP, height, plans), F32),
                pltpu.VMEM((plans, spots), F32),
                pltpu.VMEM((spots, plans), F32),
            ],
        ),
        out_shape=outs,
        compiler_params=pltpu.CompilerParams(
            vmem_limit_bytes=LARGE, dimension_semantics=("arbitrary",)
        ),
        cost_estimate=pl.CostEstimate(
            flops=2 * matrix.size * plans * 4, bytes_accessed=matrix.size * 4, transcendentals=0
        ),
        name="warp_back_and_gradient",
    )(*scalars, *([matrix] * CAP), *([warp_tiles] * CAP), *returned)


def place_body(vox, which_ref, slot_ref, *refs):
    incoming, (give, keep, total) = refs[:vox], refs[vox:]
    total[...] = jnp.zeros_like(total)
    for m in range(vox):
        for j in range(CAP):
            slot = slot_ref[m * CAP + j]

            @pl.when(slot >= 0)
            def _():
                total[slot] += incoming[m][j]

    half = keep.shape[0]
    which = which_ref[0]
    keep[...] = total[pl.ds(which * half, half)]
    give[...] = total[pl.ds((1 - which) * half, half)]


def place(which, slots, incoming, blocks):
    vox = len(incoming)
    _, height, plans = incoming[0].shape
    half = jax.ShapeDtypeStruct((blocks // 2, height, plans), F32)
    smem = pl.BlockSpec(memory_space=pltpu.SMEM)
    vmem = pl.BlockSpec(memory_space=pltpu.VMEM)
    return pl.pallas_call(
        functools.partial(place_body, vox),
        in_specs=[smem, smem] + [vmem] * vox,
        out_specs=[vmem, vmem],
        out_shape=[half, half],
        scratch_shapes=[pltpu.VMEM((blocks, height, plans), F32)],
        compiler_params=pltpu.CompilerParams(vmem_limit_bytes=SMALL),
        name="place_blocks",
    )(which, slots, *incoming)


def pull_body(vox, with_dose, which_ref, slot_ref, mine, other, goal, scale, *refs):
    half = mine.shape[0]
    which = which_ref[0]
    field = refs[-1]
    field[pl.ds(which * half, half)] = mine[...]
    field[pl.ds((1 - which) * half, half)] = other[...]
    for m in range(vox):
        for j in range(CAP):
            slot = jnp.maximum(slot_ref[m * CAP + j], 0)
            refs[m][j] = scale[slot] * (field[slot] - goal[slot])
    if with_dose:
        refs[vox][...] = field[...]


def pull(which, slots, mine, other, goal, scale, vox, with_dose):
    half, height, plans = mine.shape
    smem = pl.BlockSpec(memory_space=pltpu.SMEM)
    vmem = pl.BlockSpec(memory_space=pltpu.VMEM)
    outs = [jax.ShapeDtypeStruct((CAP, height, plans), F32)] * vox
    if with_dose:
        outs = outs + [jax.ShapeDtypeStruct((2 * half, height, plans), F32)]
    return pl.pallas_call(
        functools.partial(pull_body, vox, with_dose),
        in_specs=[smem, smem] + [vmem] * 4,
        out_specs=[vmem] * len(outs),
        out_shape=outs,
        scratch_shapes=[pltpu.VMEM((2 * half, height, plans), F32)],
        compiler_params=pltpu.CompilerParams(vmem_limit_bytes=SMALL),
        name="adjoint_blocks",
    )(which, slots, mine, other, goal, scale)


def gather_weights(shard, extra):
    phases, vox = lax.axis_size(PHASE), lax.axis_size(VOX)
    by_phase = spread(shard, PHASE, range(1, phases))
    if extra is not None:
        by_phase.append(extra)
    by_phase = jnp.concatenate(by_phase, axis=0)
    cores = core_count()
    by_chip = jnp.stack(spread(by_phase, VOX, range(cores, vox, cores)))
    return spread(by_chip, VOX, range(1, cores))


def scatter_sum(parts):
    cores = len(parts)
    chips = parts[0]
    for m in range(1, cores):
        chips = chips + swap(parts[m], VOX, m)
    mine = chips[0]
    for m in range(1, chips.shape[0]):
        mine = mine + swap(chips[m], VOX, m * cores)
    total = mine[0]
    for m in range(1, mine.shape[0]):
        total = total + swap(mine[m], PHASE, m)
    return total


def exchange(pieces):
    return [pieces[0]] + [swap(pieces[m], VOX, m) for m in range(1, len(pieces))]


def phase_halves(give, keep):
    phases = lax.axis_size(PHASE)
    if phases == 1:
        return keep, give
    keep = keep + swap(give, PHASE, 1)
    span = 4
    while span <= phases:
        keep = keep + swap(keep, PHASE, span - 1)
        span *= 2
    return keep, swap(keep, PHASE, 1)


def per_device(
    influence,
    weights,
    warp_tiles,
    owners,
    owner_slot,
    tile_index,
    structure,
    prescribed,
    importance,
    step_size,
):
    highest = lax.Precision.HIGHEST
    matrix = influence[0]
    vox_rows, spots = matrix.shape
    block_rows = warp_tiles.shape[1]
    rows, plans = weights.shape
    local_blocks = vox_rows // block_rows
    vox = lax.axis_size(VOX)
    phases = lax.axis_size(PHASE)
    cores = core_count()
    me_vox = lax.axis_index(VOX)
    me_phase = lax.axis_index(PHASE)
    slots_all = vox * CAP
    part = block_rows // CHUNKS
    targets = owners[0, :, 0]
    which = ((me_phase ^ (me_phase >> 1)) & 1).astype(jnp.int32).reshape(1)

    def orders(names):
        before = jnp.tril(jnp.ones((local_blocks, local_blocks), jnp.int32), -1)
        same = (names[..., :, None] == names[..., None, :]).astype(jnp.int32)
        return jnp.sum(same * before, axis=-1)

    position = (targets ^ me_vox) * CAP + orders(targets)
    chosen_mask = jnp.arange(slots_all, dtype=jnp.int32)[:, None] == position[None, :]
    positions_i = jnp.arange(local_blocks, dtype=jnp.int32)
    source = jnp.sum(jnp.where(chosen_mask, positions_i[None, :], 0), axis=1)
    valid = jnp.sum(chosen_mask.astype(jnp.int32), axis=1)
    tiles = jnp.sum(jnp.where(chosen_mask, tile_index[0][None, :], 0), axis=1)
    me = jnp.stack([me_vox, me_phase]).astype(jnp.int32)
    scalars = (source, valid, tiles, me)
    labels = jnp.zeros((LABEL_ROWS, plans), F32)
    labels = labels.at[0, :local_blocks].set(targets.astype(F32))
    labels = labels.at[1, :local_blocks].set(owner_slot[0].astype(F32))

    member = (structure[:, None] == jnp.arange(NSTRUCT, dtype=jnp.int32)[None, :]).astype(F32)
    target_dose = jnp.dot(member, prescribed, precision=highest, preferred_element_type=F32)
    voxel_weight = jnp.dot(
        member, importance[:, None], precision=highest, preferred_element_type=F32
    )
    voxel_weight = jnp.broadcast_to(voxel_weight, target_dose.shape)
    goals = target_dose.reshape(local_blocks, CHUNKS, part, plans)
    scales = voxel_weight.reshape(local_blocks, CHUNKS, part, plans)
    goals = [goals[:, h] for h in range(CHUNKS)]
    scales = [scales[:, h] for h in range(CHUNKS)]

    new_weights = weights
    received = None
    for iteration in range(ITERS):
        last = iteration == ITERS - 1
        pieces = gather_weights(new_weights, labels if iteration == 0 else None)
        if iteration == 0:
            infos = jnp.stack(pieces, axis=1).reshape(vox, -1, plans)[:, phases * rows :]
            names = infos[:, 0, :local_blocks].astype(jnp.int32)
            slots = infos[:, 1, :local_blocks].astype(jnp.int32)
            order = jnp.where(names == me_vox, orders(names), -1)
            hit = order[:, None, :] == jnp.arange(CAP, dtype=jnp.int32)[None, :, None]
            received = jnp.sum(jnp.where(hit, slots[:, None, :] + 1, 0), axis=-1)
            received = received.reshape(slots_all) - 1
        if rows % 16:
            every = jnp.stack(pieces, axis=1).reshape(vox, -1, plans)[:, : phases * rows]
            every = every.reshape(vox, phases, rows, plans)
            every = every[jnp.arange(vox) ^ me_vox][:, jnp.arange(phases) ^ me_phase]
            pieces = [every.transpose(1, 0, 2, 3).reshape(spots, plans)]
        outgoing = forward(scalars, matrix, warp_tiles, pieces, rows, vox, phases)
        returned, dose = [], []
        incoming = [exchange(outgoing[h * vox : (h + 1) * vox]) for h in range(CHUNKS)]
        for h in range(CHUNKS):
            give, keep = place(which, received, incoming[h], local_blocks)
            mine, other = phase_halves(give, keep)
            back = pull(which, received, mine, other, goals[h], scales[h], vox, last)
            returned += exchange(back[:vox])
            dose += back[vox:]
        parts = gradient_parts(scalars, matrix, warp_tiles, returned, rows, vox, phases)
        if rows % 8:
            parts = parts[0].reshape(phases, vox, rows, plans)
            parts = parts[jnp.arange(phases) ^ me_phase][:, jnp.arange(vox) ^ me_vox]
            parts = parts.transpose(1, 0, 2, 3).reshape(vox // cores, cores, phases, rows, plans)
            parts = [parts[:, c] for c in range(cores)]
        total = scatter_sum(parts)
        new_weights = jnp.maximum(new_weights - step_size[None, :] * total, 0.0)
    dose_field = jnp.stack(dose, axis=1).reshape(vox_rows, plans)
    return (new_weights, dose_field)


def solution(mesh):
    in_specs = (
        P("phase", "vox", None),
        P(("phase", "vox"), None),
        P(),
        P("phase", "vox", None),
        P("phase", "vox"),
        P("phase", "vox"),
        P("vox"),
        P(),
        P(),
        P(),
    )
    out_specs = (P(("phase", "vox"), None), P("vox", None))
    return jax.shard_map(
        per_device, mesh=mesh, in_specs=in_specs, out_specs=out_specs, check_vma=False
    )
```

```python
import functools

import jax
import jax.numpy as jnp
from jax import lax
from jax.experimental import pallas as pl
from jax.experimental.pallas import tpu as pltpu
from jax.sharding import PartitionSpec as P

CAP = 2
NSTRUCT = 8
ITERS = 2
CHUNKS = 2
VOX = "vox"
PHASE = "phase"
LABEL_ROWS = 16
F32 = jnp.float32
BF16 = jnp.bfloat16
LARGE = 28 << 20
SMALL = 8 << 20
ROWS_AT_ONCE = 1024
COLUMNS_AT_ONCE = 512


def swap(x, axis, mask):
    count = lax.axis_size(axis)
    return lax.ppermute(x, axis, [(i, i ^ mask) for i in range(count)])


def spread(x, axis, masks):
    return [x] + [swap(x, axis, m) for m in masks]


def core_count():
    return min(2, lax.axis_size(VOX))


def halves(x, axis):
    big = x.astype(BF16)
    small = (x - big.astype(F32)).astype(BF16)
    return jnp.concatenate([big, small], axis=axis)


def term_sum(full, rows, cols):
    return full[:rows, :cols] + (full[:rows, cols:] + full[rows:, :cols])


def split_body(tile_ref, matrix, tiles, big, small, own, buffer, tile_buffer, sems, tile_sems):
    count, height, width = own.shape[0], buffer.shape[1], matrix.shape[1]
    steps = matrix.shape[0] // height

    def fetch(i):
        return pltpu.make_async_copy(
            matrix.at[pl.ds(i * height, height)], buffer.at[i % 2], sems.at[i % 2]
        )

    def fetch_tile(b):
        return pltpu.make_async_copy(tiles.at[tile_ref[b]], tile_buffer.at[b], tile_sems.at[b])

    fetch(0).start()
    for b in range(count):
        fetch_tile(b).start()
    for i in range(steps):
        fetch(i).wait()
        if i + 1 < steps:
            fetch(i + 1).start()
        x = buffer[i % 2]
        top = x.astype(BF16)
        big[i * height : (i + 1) * height, :] = top
        small[i * height : (i + 1) * height, :] = (x - top.astype(F32)).astype(BF16)
    for b in range(count):
        fetch_tile(b).wait()
        own[b] = halves(tile_buffer[b], 1)


def specs(count, space):
    return [pl.BlockSpec(memory_space=space)] * count


def split_terms(tile_index, matrix, warp_tiles, blocks):
    height, width = warp_tiles.shape[1:]
    step = 2 * height
    terms = jax.ShapeDtypeStruct(matrix.shape, BF16)
    return pl.pallas_call(
        split_body,
        in_specs=specs(1, pltpu.SMEM) + specs(2, pltpu.HBM),
        out_specs=specs(3, pltpu.VMEM),
        out_shape=[terms, terms, jax.ShapeDtypeStruct((blocks, height, 2 * width), BF16)],
        scratch_shapes=[
            pltpu.VMEM((2, step, matrix.shape[1]), F32),
            pltpu.VMEM((blocks, height, width), F32),
            pltpu.SemaphoreType.DMA((2,)),
            pltpu.SemaphoreType.DMA((blocks,)),
        ],
        compiler_params=pltpu.CompilerParams(vmem_limit_bytes=LARGE),
        cost_estimate=pl.CostEstimate(
            flops=matrix.size, bytes_accessed=matrix.size * 4, transcendentals=0
        ),
        name="split_terms",
    )(tile_index, matrix, warp_tiles)


def fill_weights(me_ref, out, pieces, rows, vox, masks):
    cores = len(pieces)
    for c, ref in enumerate(pieces):
        for k in range(vox // cores):
            for i, p in enumerate(masks):
                v = me_ref[0] ^ (k * cores + c)
                at = ((me_ref[1] ^ p) * vox + v) * rows
                out[pl.ds(pl.multiple_of(at, rows), rows), :] = halves(
                    ref[k, i * rows : (i + 1) * rows, :], 1
                )


def forward_body(dims, source_ref, valid_ref, me_ref, big, small, tiles, *refs):
    vox, masks, rows, pieces_n, chunks = dims
    pieces, outs = refs[:pieces_n], refs[pieces_n:-2]
    weights, dose = refs[-2:]
    plans = dose.shape[1]
    height = tiles.shape[1]
    if len(pieces[0].shape) == 2:
        weights[...] = halves(pieces[0][...], 1)
    else:
        fill_weights(me_ref, weights, pieces, rows, vox, masks)
    step = min(ROWS_AT_ONCE, dose.shape[0])

    def multiply(i, carry):
        at = pl.ds(pl.multiple_of(i * step, step), step)
        top = jnp.dot(big[at, :], weights[...], preferred_element_type=F32)
        rest = jnp.dot(small[at, :], weights[:, :plans], preferred_element_type=F32)
        dose[at, :] = top[:, :plans] + (top[:, plans:] + rest)
        return carry

    lax.fori_loop(0, dose.shape[0] // step, multiply, 0)
    part = height // chunks
    for m in range(vox):
        for j in range(CAP):
            s = m * CAP + j
            b = source_ref[s]
            block = dose[pl.ds(pl.multiple_of(b * height, height), height), :]
            tile = tiles[b]
            left = jnp.concatenate([tile[:, :height], tile[:, height:]], axis=0)
            full = jnp.dot(left, halves(block, 1), preferred_element_type=F32)
            warped = jnp.where(valid_ref[s] > 0, term_sum(full, height, plans), 0.0)
            for h in range(chunks):
                outs[h * vox + m][j] = warped[h * part : (h + 1) * part]


def forward(scalars, terms, pieces, rows, vox, masks):
    big, small, tiles = terms
    height = tiles.shape[1]
    vox_rows, spots = big.shape
    plans = pieces[0].shape[-1]
    out = jax.ShapeDtypeStruct((CAP, height // CHUNKS, plans), F32)
    return pl.pallas_call(
        functools.partial(forward_body, (vox, masks, rows, len(pieces), CHUNKS)),
        in_specs=specs(3, pltpu.SMEM) + specs(3 + len(pieces), pltpu.VMEM),
        out_specs=specs(vox * CHUNKS, pltpu.VMEM),
        out_shape=[out] * (vox * CHUNKS),
        scratch_shapes=[pltpu.VMEM((spots, 2 * plans), BF16), pltpu.VMEM((vox_rows, plans), F32)],
        compiler_params=pltpu.CompilerParams(vmem_limit_bytes=LARGE),
        cost_estimate=pl.CostEstimate(
            flops=8 * big.size * plans, bytes_accessed=big.size * 4, transcendentals=0
        ),
        name="dose_and_warp",
    )(*scalars, *terms, *pieces)


def gradient_body(dims, source_ref, valid_ref, me_ref, big, small, tiles, *refs):
    vox, masks, rows, cores, chunks = dims
    returned = refs[: vox * chunks]
    outs = refs[vox * chunks : -2]
    columns, turned = refs[-2:]
    height = tiles.shape[1]
    plans = turned.shape[1]
    spots = big.shape[1]
    for m in range(vox):
        for j in range(CAP):
            s = m * CAP + j

            @pl.when(valid_ref[s] > 0)
            def _():
                b = source_ref[s]
                adjoint = jnp.concatenate([returned[h * vox + m][j] for h in range(chunks)], axis=0)
                full = jnp.dot(halves(adjoint.T, 0), tiles[b], preferred_element_type=F32)
                at = pl.ds(pl.multiple_of(b * height, height), height)
                columns[:, at] = halves(term_sum(full, plans, height), 0)

    for first in range(0, spots, COLUMNS_AT_ONCE):
        last = min(first + COLUMNS_AT_ONCE, spots)
        top = jnp.dot(columns[...], big[:, first:last], preferred_element_type=F32)
        rest = jnp.dot(columns[:plans, :], small[:, first:last], preferred_element_type=F32)
        total = top[:plans] + (top[plans:] + rest)
        for i in range(0, last - first, plans):
            turned[first + i : first + i + plans, :] = total[:, i : i + plans].T
    if len(outs[0].shape) == 2:
        outs[0][...] = turned[...]
    else:
        for c in range(cores):
            for k in range(vox // cores):
                for i, p in enumerate(masks):
                    v = me_ref[0] ^ (k * cores + c)
                    at = ((me_ref[1] ^ p) * vox + v) * rows
                    outs[c][k, i * rows : (i + 1) * rows] = turned[
                        pl.ds(pl.multiple_of(at, rows), rows), :
                    ]


def gradient_parts(scalars, terms, returned, rows, vox, masks):
    big, small, tiles = terms
    vox_rows, spots = big.shape
    plans = returned[0].shape[-1]
    cores = core_count()
    if rows % 8 == 0:
        outs = [jax.ShapeDtypeStruct((vox // cores, len(masks) * rows, plans), F32)] * cores
    else:
        outs = [jax.ShapeDtypeStruct((spots, plans), F32)]
    return pl.pallas_call(
        functools.partial(gradient_body, (vox, masks, rows, cores, CHUNKS)),
        in_specs=specs(3, pltpu.SMEM) + specs(3 + len(returned), pltpu.VMEM),
        out_specs=specs(len(outs), pltpu.VMEM),
        out_shape=outs,
        scratch_shapes=[pltpu.VMEM((2 * plans, vox_rows), BF16), pltpu.VMEM((spots, plans), F32)],
        compiler_params=pltpu.CompilerParams(vmem_limit_bytes=LARGE),
        cost_estimate=pl.CostEstimate(
            flops=8 * big.size * plans, bytes_accessed=big.size * 4, transcendentals=0
        ),
        name="warp_back_and_gradient",
    )(*scalars, *terms, *returned)


def place_body(vox, which_ref, slot_ref, *refs):
    incoming, (give, keep, total) = refs[:vox], refs[vox:]
    total[...] = jnp.zeros_like(total)
    for m in range(vox):
        for j in range(CAP):
            slot = slot_ref[m * CAP + j]

            @pl.when(slot >= 0)
            def _():
                total[slot] += incoming[m][j]

    half = keep.shape[0]
    which = which_ref[0]
    keep[...] = total[pl.ds(which * half, half)]
    give[...] = total[pl.ds((1 - which) * half, half)]


def place(which, slots, incoming, blocks):
    vox = len(incoming)
    _, height, plans = incoming[0].shape
    half = jax.ShapeDtypeStruct((blocks // 2, height, plans), F32)
    smem = pl.BlockSpec(memory_space=pltpu.SMEM)
    vmem = pl.BlockSpec(memory_space=pltpu.VMEM)
    return pl.pallas_call(
        functools.partial(place_body, vox),
        in_specs=[smem, smem] + [vmem] * vox,
        out_specs=[vmem, vmem],
        out_shape=[half, half],
        scratch_shapes=[pltpu.VMEM((blocks, height, plans), F32)],
        compiler_params=pltpu.CompilerParams(vmem_limit_bytes=SMALL),
        name="place_blocks",
    )(which, slots, *incoming)


def pull_body(vox, with_dose, which_ref, slot_ref, mine, other, goal, scale, *refs):
    half = mine.shape[0]
    which = which_ref[0]
    field = refs[-1]
    field[pl.ds(which * half, half)] = mine[...]
    field[pl.ds((1 - which) * half, half)] = other[...]
    for m in range(vox):
        for j in range(CAP):
            slot = jnp.maximum(slot_ref[m * CAP + j], 0)
            refs[m][j] = scale[slot] * (field[slot] - goal[slot])
    if with_dose:
        refs[vox][...] = field[...]


def pull(which, slots, mine, other, goal, scale, vox, with_dose):
    half, height, plans = mine.shape
    smem = pl.BlockSpec(memory_space=pltpu.SMEM)
    vmem = pl.BlockSpec(memory_space=pltpu.VMEM)
    outs = [jax.ShapeDtypeStruct((CAP, height, plans), F32)] * vox
    if with_dose:
        outs = outs + [jax.ShapeDtypeStruct((2 * half, height, plans), F32)]
    return pl.pallas_call(
        functools.partial(pull_body, vox, with_dose),
        in_specs=[smem, smem] + [vmem] * 4,
        out_specs=[vmem] * len(outs),
        out_shape=outs,
        scratch_shapes=[pltpu.VMEM((2 * half, height, plans), F32)],
        compiler_params=pltpu.CompilerParams(vmem_limit_bytes=SMALL),
        name="adjoint_blocks",
    )(which, slots, mine, other, goal, scale)


def phase_steps():
    count, steps = lax.axis_size(PHASE), []
    while 2 ** len(steps) < count:
        steps.append(2 ** (len(steps) + 1) - 1)
    return steps


def chip_steps():
    count, steps, mask = lax.axis_size(VOX), [], core_count()
    while mask < count:
        steps.append(mask)
        mask *= 2
    return steps


def combined(steps):
    masks = [0]
    for s in steps:
        masks += [m ^ s for m in masks]
    return masks


def gather_along(x, axis, steps, backwards=False):
    out = x[None]
    for s in reversed(steps) if backwards else steps:
        other = swap(out, axis, s)
        out = jnp.stack([out, other], axis=1 if backwards else 0).reshape(-1, *x.shape)
    return out


def sum_along(x, axis, steps, backwards=False):
    for s in reversed(steps) if backwards else steps:
        pairs = x.reshape(2, -1, *x.shape[1:]) if backwards else x.reshape(-1, 2, *x.shape[1:])
        keep, give = (pairs[0], pairs[1]) if backwards else (pairs[:, 0], pairs[:, 1])
        x = keep + swap(give, axis, s)
    return x


def sum_everywhere(x, axis, steps):
    for i, s in enumerate(steps):
        other = swap(x, axis, s).reshape(-1, 2, 2**i, *x.shape[1:])
        x = x + jnp.concatenate([other[:, 1:], other[:, :1]], axis=1).reshape(x.shape)
    return x


def gather_chips(by_phase):
    half = by_phase.shape[0] // 2
    by_chip = jnp.concatenate(
        [
            gather_along(by_phase[:half], VOX, chip_steps()),
            gather_along(by_phase[half:], VOX, chip_steps(), True),
        ],
        axis=1,
    )
    return spread(by_chip, VOX, range(1, core_count()))


def sum_chips(parts):
    chips = parts[0]
    for m in range(1, len(parts)):
        chips = chips + swap(parts[m], VOX, m)
    half = chips.shape[1] // 2
    first = sum_along(chips[:, :half], VOX, chip_steps())
    second = sum_along(chips[:, half:], VOX, chip_steps(), True)
    return jnp.concatenate([first[0], second[0]], axis=0)


def exchange(pieces):
    return [pieces[0]] + [swap(pieces[m], VOX, m) for m in range(1, len(pieces))]


def phase_halves(give, keep):
    phases = lax.axis_size(PHASE)
    if phases == 1:
        return keep, give
    keep = keep + swap(give, PHASE, 1)
    span = 4
    while span <= phases:
        keep = keep + swap(keep, PHASE, span - 1)
        span *= 2
    return keep, swap(keep, PHASE, 1)


def per_device(
    influence,
    weights,
    warp_tiles,
    owners,
    owner_slot,
    tile_index,
    structure,
    prescribed,
    importance,
    step_size,
):
    highest = lax.Precision.HIGHEST
    matrix = influence[0]
    vox_rows, spots = matrix.shape
    block_rows = warp_tiles.shape[1]
    rows, plans = weights.shape
    local_blocks = vox_rows // block_rows
    vox = lax.axis_size(VOX)
    phases = lax.axis_size(PHASE)
    cores = core_count()
    me_vox = lax.axis_index(VOX)
    me_phase = lax.axis_index(PHASE)
    slots_all = vox * CAP
    part = block_rows // CHUNKS
    targets = owners[0, :, 0]
    which = ((me_phase ^ (me_phase >> 1)) & 1).astype(jnp.int32).reshape(1)

    def orders(names):
        before = jnp.tril(jnp.ones((local_blocks, local_blocks), jnp.int32), -1)
        same = (names[..., :, None] == names[..., None, :]).astype(jnp.int32)
        return jnp.sum(same * before, axis=-1)

    position = (targets ^ me_vox) * CAP + orders(targets)
    chosen_mask = jnp.arange(slots_all, dtype=jnp.int32)[:, None] == position[None, :]
    positions_i = jnp.arange(local_blocks, dtype=jnp.int32)
    source = jnp.sum(jnp.where(chosen_mask, positions_i[None, :], 0), axis=1)
    valid = jnp.sum(chosen_mask.astype(jnp.int32), axis=1)
    me = jnp.stack([me_vox, me_phase]).astype(jnp.int32)
    scalars = (source, valid, me)
    labels = jnp.zeros((LABEL_ROWS, plans), F32)
    labels = labels.at[0, :local_blocks].set(targets.astype(F32))
    labels = labels.at[1, :local_blocks].set(owner_slot[0].astype(F32))

    member = (structure[:, None] == jnp.arange(NSTRUCT, dtype=jnp.int32)[None, :]).astype(F32)
    target_dose = jnp.dot(member, prescribed, precision=highest, preferred_element_type=F32)
    voxel_weight = jnp.dot(
        member, importance[:, None], precision=highest, preferred_element_type=F32
    )
    voxel_weight = jnp.broadcast_to(voxel_weight, target_dose.shape)
    goals = target_dose.reshape(local_blocks, CHUNKS, part, plans)
    scales = voxel_weight.reshape(local_blocks, CHUNKS, part, plans)
    goals = [goals[:, h] for h in range(CHUNKS)]
    scales = [scales[:, h] for h in range(CHUNKS)]

    masks = combined(phase_steps())
    terms = split_terms(tile_index[0], matrix, warp_tiles, local_blocks)
    held = gather_along(weights, PHASE, phase_steps()).reshape(-1, plans)
    for iteration in range(ITERS):
        last = iteration == ITERS - 1
        if iteration == 0:
            pieces = gather_chips(jnp.concatenate([held, labels], axis=0))
            infos = jnp.stack(pieces, axis=1).reshape(vox, -1, plans)[:, phases * rows :]
            names = infos[:, 0, :local_blocks].astype(jnp.int32)
            slots = infos[:, 1, :local_blocks].astype(jnp.int32)
            order = jnp.where(names == me_vox, orders(names), -1)
            hit = order[:, None, :] == jnp.arange(CAP, dtype=jnp.int32)[None, :, None]
            received = jnp.sum(jnp.where(hit, slots[:, None, :] + 1, 0), axis=-1)
            received = received.reshape(slots_all) - 1
        else:
            pieces = gather_chips(held)
        if rows % 16:
            every = jnp.stack(pieces, axis=1).reshape(vox, -1, plans)[:, : phases * rows]
            every = every.reshape(vox, phases, rows, plans)
            back_to = jnp.asarray([masks.index(p) for p in range(phases)], jnp.int32)
            every = every[jnp.arange(vox) ^ me_vox][:, back_to[jnp.arange(phases) ^ me_phase]]
            pieces = [every.transpose(1, 0, 2, 3).reshape(spots, plans)]
        outgoing = forward(scalars, terms, pieces, rows, vox, masks)
        returned, dose = [], []
        incoming = [exchange(outgoing[h * vox : (h + 1) * vox]) for h in range(CHUNKS)]
        for h in range(CHUNKS):
            give, keep = place(which, received, incoming[h], local_blocks)
            mine, other = phase_halves(give, keep)
            back = pull(which, received, mine, other, goals[h], scales[h], vox, last)
            returned += exchange(back[:vox])
            dose += back[vox:]
        parts = gradient_parts(scalars, terms, returned, rows, vox, masks)
        if rows % 8:
            parts = parts[0].reshape(phases, vox, rows, plans)
            wanted = jnp.asarray(masks, jnp.int32) ^ me_phase
            parts = parts[wanted][:, jnp.arange(vox) ^ me_vox]
            parts = parts.transpose(1, 0, 2, 3).reshape(vox // cores, cores, phases * rows, plans)
            parts = [parts[:, c] for c in range(cores)]
        total = sum_chips(parts)
        if last:
            total = sum_along(total.reshape(phases, rows, plans), PHASE, phase_steps())[0]
            new_weights = jnp.maximum(held[:rows] - step_size[None, :] * total, 0.0)
        else:
            total = sum_everywhere(total.reshape(phases, rows, plans), PHASE, phase_steps())
            held = jnp.maximum(held - step_size[None, :] * total.reshape(held.shape), 0.0)
    dose_field = jnp.stack(dose, axis=1).reshape(vox_rows, plans)
    return (new_weights, dose_field)


def solution(mesh):
    in_specs = (
        P("phase", "vox", None),
        P(("phase", "vox"), None),
        P(),
        P("phase", "vox", None),
        P("phase", "vox"),
        P("phase", "vox"),
        P("vox"),
        P(),
        P(),
        P(),
    )
    out_specs = (P(("phase", "vox"), None), P("vox", None))
    return jax.shard_map(
        per_device, mesh=mesh, in_specs=in_specs, out_specs=out_specs, check_vma=False
    )
```

```python
import functools

import jax
import jax.numpy as jnp
from jax import lax
from jax.experimental import pallas as pl
from jax.experimental.pallas import tpu as pltpu
from jax.sharding import PartitionSpec as P

CAP = 2
NSTRUCT = 8
ITERS = 2
CHUNKS = 2
VOX = "vox"
PHASE = "phase"
LABEL_ROWS = 16
F32 = jnp.float32
BF16 = jnp.bfloat16
LARGE = 14 << 20
SMALL = 4 << 20
ROWS_AT_ONCE = 1024
COLUMNS_AT_ONCE = 512
FETCHES = 4


def swap(x, axis, mask):
    count = lax.axis_size(axis)
    return lax.ppermute(x, axis, [(i, i ^ mask) for i in range(count)])


def spread(x, axis, masks):
    return [x] + [swap(x, axis, m) for m in masks]


def core_count():
    return min(2, lax.axis_size(VOX))


def halves(x, axis):
    big = x.astype(BF16)
    small = (x - big.astype(F32)).astype(BF16)
    return jnp.concatenate([big, small], axis=axis)


def term_sum(full, rows, cols):
    return full[:rows, :cols] + (full[:rows, cols:] + full[rows:, :cols])


def split_body(tile_ref, matrix, tiles, big, small, own, buffer, tile_buffer, sems, tile_sems):
    count, height, width = own.shape[0], buffer.shape[1], matrix.shape[1]
    steps = matrix.shape[0] // height

    depth = buffer.shape[0]

    def fetch(i):
        return pltpu.make_async_copy(
            matrix.at[pl.ds(i * height, height)], buffer.at[i % depth], sems.at[i % depth]
        )

    def fetch_tile(b):
        return pltpu.make_async_copy(tiles.at[tile_ref[b]], tile_buffer.at[b], tile_sems.at[b])

    for i in range(min(depth - 1, steps)):
        fetch(i).start()
    for b in range(count):
        fetch_tile(b).start()
    for i in range(steps):
        fetch(i).wait()
        if i + depth - 1 < steps:
            fetch(i + depth - 1).start()
        x = buffer[i % depth]
        top = x.astype(BF16)
        big[i * height : (i + 1) * height, :] = top
        small[i * height : (i + 1) * height, :] = (x - top.astype(F32)).astype(BF16)
    for b in range(count):
        fetch_tile(b).wait()
        own[b] = halves(tile_buffer[b], 1)


def specs(count, space):
    return [pl.BlockSpec(memory_space=space)] * count


def split_terms(tile_index, matrix, warp_tiles, blocks):
    height, width = warp_tiles.shape[1:]
    step = 2 * height
    terms = jax.ShapeDtypeStruct(matrix.shape, BF16)
    return pl.pallas_call(
        split_body,
        in_specs=specs(1, pltpu.SMEM) + specs(2, pltpu.HBM),
        out_specs=specs(3, pltpu.VMEM),
        out_shape=[terms, terms, jax.ShapeDtypeStruct((blocks, height, 2 * width), BF16)],
        scratch_shapes=[
            pltpu.VMEM((FETCHES, step, matrix.shape[1]), F32),
            pltpu.VMEM((blocks, height, width), F32),
            pltpu.SemaphoreType.DMA((FETCHES,)),
            pltpu.SemaphoreType.DMA((blocks,)),
        ],
        compiler_params=pltpu.CompilerParams(vmem_limit_bytes=LARGE),
        cost_estimate=pl.CostEstimate(
            flops=matrix.size, bytes_accessed=matrix.size * 4, transcendentals=0
        ),
        name="split_terms",
    )(tile_index, matrix, warp_tiles)


def fill_weights(me_ref, out, pieces, rows, vox, masks):
    cores = len(pieces)
    for c, ref in enumerate(pieces):
        for k in range(vox // cores):
            for i, p in enumerate(masks):
                v = me_ref[0] ^ (k * cores + c)
                at = ((me_ref[1] ^ p) * vox + v) * rows
                out[pl.ds(pl.multiple_of(at, rows), rows), :] = halves(
                    ref[k, i * rows : (i + 1) * rows, :], 1
                )


def warp_chunk(h, chunks, cores, source_ref, valid_ref, tiles, dose, outs):
    height = tiles.shape[1]
    part = height // chunks
    for k, out in enumerate(outs):
        for c in range(cores):
            for j in range(CAP):
                s = (k * cores + c) * CAP + j
                b = source_ref[s]
                block = dose[pl.ds(pl.multiple_of(b * height, height), height), :]
                tile = tiles[b, h * part : (h + 1) * part, :]
                left = jnp.concatenate([tile[:, :height], tile[:, height:]], axis=0)
                full = jnp.dot(left, halves(block, 1), preferred_element_type=F32)
                warped = term_sum(full, part, dose.shape[1])
                out[c, j] = jnp.where(valid_ref[s] > 0, warped, 0.0)


def forward_body(dims, source_ref, valid_ref, me_ref, big, small, tiles, *refs):
    vox, masks, rows, pieces_n, chunks, cores = dims
    pieces, outs = refs[:pieces_n], refs[pieces_n:-2]
    dose, weights = refs[-2:]
    plans = dose.shape[1]
    if len(pieces[0].shape) == 2:
        weights[...] = halves(pieces[0][...], 1)
    else:
        fill_weights(me_ref, weights, pieces, rows, vox, masks)
    step = min(ROWS_AT_ONCE, dose.shape[0])
    for first in range(0, dose.shape[0], step):
        at = slice(first, first + step)
        top = jnp.dot(big[at, :], weights[...], preferred_element_type=F32)
        rest = jnp.dot(small[at, :], weights[:, :plans], preferred_element_type=F32)
        dose[at, :] = top[:, :plans] + (top[:, plans:] + rest)
    warp_chunk(0, chunks, cores, source_ref, valid_ref, tiles, dose, outs)


def forward(scalars, terms, pieces, rows, vox, masks):
    big, small, tiles = terms
    height = tiles.shape[1]
    vox_rows, spots = big.shape
    plans = pieces[0].shape[-1]
    cores = core_count()
    out = jax.ShapeDtypeStruct((cores, CAP, height // CHUNKS, plans), F32)
    outs = [out] * (vox // cores) + [jax.ShapeDtypeStruct((vox_rows, plans), F32)]
    return pl.pallas_call(
        functools.partial(forward_body, (vox, masks, rows, len(pieces), CHUNKS, cores)),
        in_specs=specs(3, pltpu.SMEM) + specs(3 + len(pieces), pltpu.VMEM),
        out_specs=specs(len(outs), pltpu.VMEM),
        out_shape=outs,
        scratch_shapes=[pltpu.VMEM((spots, 2 * plans), BF16)],
        compiler_params=pltpu.CompilerParams(vmem_limit_bytes=LARGE),
        cost_estimate=pl.CostEstimate(
            flops=8 * big.size * plans, bytes_accessed=big.size * 4, transcendentals=0
        ),
        name="dose_and_warp",
    )(*scalars, *terms, *pieces)


def later_body(h, chunks, cores, source_ref, valid_ref, tiles, dose, after, *outs):
    warp_chunk(h, chunks, cores, source_ref, valid_ref, tiles, dose, outs)


def forward_later(h, scalars, tiles, dose, after, vox):
    height = tiles.shape[1]
    cores = core_count()
    out = jax.ShapeDtypeStruct((cores, CAP, height // CHUNKS, dose.shape[1]), F32)
    return pl.pallas_call(
        functools.partial(later_body, h, CHUNKS, cores),
        in_specs=specs(2, pltpu.SMEM) + specs(2, pltpu.VMEM) + specs(1, pl.ANY),
        out_specs=specs(vox // cores, pltpu.VMEM),
        out_shape=[out] * (vox // cores),
        compiler_params=pltpu.CompilerParams(vmem_limit_bytes=SMALL),
        name="warp_later",
    )(*scalars[:2], tiles, dose, after)


def piece(arrived, across, cores, m):
    k, c = m // cores, m % cores
    return arrived[k].at[0] if c == 0 else across[(c - 1) * len(arrived) + k]


def gradient_body(dims, source_ref, valid_ref, me_ref, big, small, tiles, *refs):
    vox, masks, rows, cores, chunks = dims
    chips = vox // cores
    each = chips * cores
    returned = refs[: each * chunks]
    outs = refs[each * chunks : -2]
    columns, turned = refs[-2:]
    height = tiles.shape[1]
    plans = turned.shape[1]
    vox_rows, spots = big.shape
    spare = vox_rows // height
    for m in range(vox):
        found = [
            piece(
                returned[h * each : h * each + chips],
                returned[h * each + chips : (h + 1) * each],
                cores,
                m,
            )
            for h in range(chunks)
        ]
        for j in range(CAP):
            s = m * CAP + j
            b = source_ref[s]
            adjoint = jnp.concatenate([f[j] for f in found], axis=0)
            full = jnp.dot(halves(adjoint.T, 0), tiles[b], preferred_element_type=F32)
            to = jnp.where(valid_ref[s] > 0, b, spare) * height
            columns[:, pl.ds(pl.multiple_of(to, height), height)] = halves(
                term_sum(full, plans, height), 0
            )

    for first in range(0, spots, COLUMNS_AT_ONCE):
        last = min(first + COLUMNS_AT_ONCE, spots)
        top = jnp.dot(columns[:, :vox_rows], big[:, first:last], preferred_element_type=F32)
        rest = jnp.dot(
            columns[:plans, :vox_rows], small[:, first:last], preferred_element_type=F32
        )
        total = top[:plans] + (top[plans:] + rest)
        for i in range(0, last - first, plans):
            turned[first + i : first + i + plans, :] = total[:, i : i + plans].T
    if len(outs[0].shape) == 2:
        outs[0][...] = turned[...]
    else:
        for c in range(cores):
            for k in range(vox // cores):
                for i, p in enumerate(masks):
                    v = me_ref[0] ^ (k * cores + c)
                    at = ((me_ref[1] ^ p) * vox + v) * rows
                    outs[c][k, i * rows : (i + 1) * rows] = turned[
                        pl.ds(pl.multiple_of(at, rows), rows), :
                    ]


def gradient_parts(scalars, terms, returned, rows, vox, masks):
    big, small, tiles = terms
    vox_rows, spots = big.shape
    plans = returned[0].shape[-1]
    cores = core_count()
    if rows % 8 == 0:
        outs = [jax.ShapeDtypeStruct((vox // cores, len(masks) * rows, plans), F32)] * cores
    else:
        outs = [jax.ShapeDtypeStruct((spots, plans), F32)]
    return pl.pallas_call(
        functools.partial(gradient_body, (vox, masks, rows, cores, CHUNKS)),
        in_specs=specs(3, pltpu.SMEM) + specs(3 + len(returned), pltpu.VMEM),
        out_specs=specs(len(outs), pltpu.VMEM),
        out_shape=outs,
        scratch_shapes=[pltpu.VMEM((2 * plans, vox_rows + tiles.shape[1]), BF16),
            pltpu.VMEM((spots, plans), F32),
        ],
        compiler_params=pltpu.CompilerParams(vmem_limit_bytes=LARGE),
        cost_estimate=pl.CostEstimate(
            flops=8 * big.size * plans, bytes_accessed=big.size * 4, transcendentals=0
        ),
        name="warp_back_and_gradient",
    )(*scalars, *terms, *returned)


def place_body(vox, cores, which_ref, slot_ref, *refs):
    chips = vox // cores
    arrived, across = refs[:chips], refs[chips:vox]
    give, keep, total = refs[vox:]
    total[...] = jnp.zeros_like(total)
    for m in range(vox):
        blocks = piece(arrived, across, cores, m)
        for j in range(CAP):
            slot = slot_ref[m * CAP + j]

            @pl.when(slot >= 0)
            def _():
                total[slot] += blocks[j]

    half = keep.shape[0]
    which = which_ref[0]
    keep[...] = total[pl.ds(which * half, half)]
    give[...] = total[pl.ds((1 - which) * half, half)]


def place(which, slots, incoming, blocks):
    vox = len(incoming)
    height, plans = incoming[0].shape[-2:]
    half = jax.ShapeDtypeStruct((blocks // 2, height, plans), F32)
    return pl.pallas_call(
        functools.partial(place_body, vox, core_count()),
        in_specs=specs(2, pltpu.SMEM) + specs(vox, pltpu.VMEM),
        out_specs=specs(2, pltpu.VMEM),
        out_shape=[half, half],
        scratch_shapes=[pltpu.VMEM((blocks, height, plans), F32)],
        compiler_params=pltpu.CompilerParams(vmem_limit_bytes=SMALL),
        name="place_blocks",
    )(which, slots, *incoming)


def pull_body(vox, cores, with_dose, which_ref, slot_ref, mine, other, goal, scale, *refs):
    half = mine.shape[0]
    which = which_ref[0]
    field = refs[-1]
    field[pl.ds(which * half, half)] = mine[...]
    field[pl.ds((1 - which) * half, half)] = other[...]
    for m in range(vox):
        for j in range(CAP):
            slot = jnp.maximum(slot_ref[m * CAP + j], 0)
            refs[m // cores][m % cores, j] = scale[slot] * (field[slot] - goal[slot])
    if with_dose:
        refs[vox // cores][...] = field[...]


def pull(which, slots, mine, other, goal, scale, vox, with_dose):
    half, height, plans = mine.shape
    cores = core_count()
    outs = [jax.ShapeDtypeStruct((cores, CAP, height, plans), F32)] * (vox // cores)
    if with_dose:
        outs = outs + [jax.ShapeDtypeStruct((2 * half, height, plans), F32)]
    return pl.pallas_call(
        functools.partial(pull_body, vox, cores, with_dose),
        in_specs=specs(2, pltpu.SMEM) + specs(4, pltpu.VMEM),
        out_specs=specs(len(outs), pltpu.VMEM),
        out_shape=outs,
        scratch_shapes=[pltpu.VMEM((2 * half, height, plans), F32)],
        compiler_params=pltpu.CompilerParams(vmem_limit_bytes=SMALL),
        name="adjoint_blocks",
    )(which, slots, mine, other, goal, scale)


def phase_steps():
    count, steps = lax.axis_size(PHASE), []
    while 2 ** len(steps) < count:
        steps.append(2 ** (len(steps) + 1) - 1)
    return steps


def combined(steps):
    masks = [0]
    for s in steps:
        masks += [m ^ s for m in masks]
    return masks


def sum_everywhere(x, axis, steps):
    for i, s in enumerate(steps):
        other = swap(x, axis, s).reshape(-1, 2, 2**i, *x.shape[1:])
        x = x + jnp.concatenate([other[:, 1:], other[:, :1]], axis=1).reshape(x.shape)
    return x


def gather_chips(by_phase):
    cores = core_count()
    by_chip = jnp.stack(spread(by_phase, VOX, range(cores, lax.axis_size(VOX), cores)))
    return spread(by_chip, VOX, range(1, cores))


def sum_chips(parts):
    cores = len(parts)
    chips = parts[0]
    for m in range(1, cores):
        chips = chips + swap(parts[m], VOX, m)
    mine = chips[0]
    for k in range(1, chips.shape[0]):
        mine = mine + swap(chips[k], VOX, k * cores)
    return mine


def exchange(pieces):
    cores = core_count()
    arrived = [pieces[0]] + [swap(pieces[k], VOX, k * cores) for k in range(1, len(pieces))]
    return arrived + [swap(a[c], VOX, c) for c in range(1, cores) for a in arrived]


def phase_halves(give, keep):
    phases = lax.axis_size(PHASE)
    if phases == 1:
        return keep, give
    keep = keep + swap(give, PHASE, 1)
    span = 4
    while span <= phases:
        keep = keep + swap(keep, PHASE, span - 1)
        span *= 2
    return keep, swap(keep, PHASE, 1)


def per_device(
    influence,
    weights,
    warp_tiles,
    owners,
    owner_slot,
    tile_index,
    structure,
    prescribed,
    importance,
    step_size,
):
    highest = lax.Precision.HIGHEST
    matrix = influence[0]
    vox_rows, spots = matrix.shape
    block_rows = warp_tiles.shape[1]
    rows, plans = weights.shape
    local_blocks = vox_rows // block_rows
    vox = lax.axis_size(VOX)
    phases = lax.axis_size(PHASE)
    cores = core_count()
    me_vox = lax.axis_index(VOX)
    me_phase = lax.axis_index(PHASE)
    slots_all = vox * CAP
    part = block_rows // CHUNKS
    targets = owners[0, :, 0]
    which = ((me_phase ^ (me_phase >> 1)) & 1).astype(jnp.int32).reshape(1)

    def orders(names):
        before = jnp.tril(jnp.ones((local_blocks, local_blocks), jnp.int32), -1)
        same = (names[..., :, None] == names[..., None, :]).astype(jnp.int32)
        return jnp.sum(same * before, axis=-1)

    position = (targets ^ me_vox) * CAP + orders(targets)
    chosen_mask = jnp.arange(slots_all, dtype=jnp.int32)[:, None] == position[None, :]
    positions_i = jnp.arange(local_blocks, dtype=jnp.int32)
    source = jnp.sum(jnp.where(chosen_mask, positions_i[None, :], 0), axis=1)
    valid = jnp.sum(chosen_mask.astype(jnp.int32), axis=1)
    me = jnp.stack([me_vox, me_phase]).astype(jnp.int32)
    scalars = (source, valid, me)
    labels = jnp.zeros((LABEL_ROWS, plans), F32)
    labels = labels.at[0, :local_blocks].set(targets.astype(F32))
    labels = labels.at[1, :local_blocks].set(owner_slot[0].astype(F32))

    member = (structure[:, None] == jnp.arange(NSTRUCT, dtype=jnp.int32)[None, :]).astype(F32)
    target_dose = jnp.dot(member, prescribed, precision=highest, preferred_element_type=F32)
    voxel_weight = jnp.dot(
        member, importance[:, None], precision=highest, preferred_element_type=F32
    )
    voxel_weight = jnp.broadcast_to(voxel_weight, target_dose.shape)
    goals = target_dose.reshape(local_blocks, CHUNKS, part, plans)
    scales = voxel_weight.reshape(local_blocks, CHUNKS, part, plans)
    goals = [goals[:, h] for h in range(CHUNKS)]
    scales = [scales[:, h] for h in range(CHUNKS)]

    masks = combined(phase_steps())
    terms = split_terms(tile_index[0], matrix, warp_tiles, local_blocks)
    held = jnp.concatenate(spread(weights, PHASE, masks[1:]), axis=0)
    for iteration in range(ITERS):
        last = iteration == ITERS - 1
        if iteration == 0:
            pieces = gather_chips(jnp.concatenate([held, labels], axis=0))
            infos = jnp.stack(pieces, axis=1).reshape(vox, -1, plans)[:, phases * rows :]
            names = infos[:, 0, :local_blocks].astype(jnp.int32)
            slots = infos[:, 1, :local_blocks].astype(jnp.int32)
            order = jnp.where(names == me_vox, orders(names), -1)
            hit = order[:, None, :] == jnp.arange(CAP, dtype=jnp.int32)[None, :, None]
            received = jnp.sum(jnp.where(hit, slots[:, None, :] + 1, 0), axis=-1)
            received = received.reshape(slots_all) - 1
        else:
            pieces = gather_chips(held)
        if rows % 16:
            every = jnp.stack(pieces, axis=1).reshape(vox, -1, plans)[:, : phases * rows]
            every = every.reshape(vox, phases, rows, plans)
            back_to = jnp.asarray([masks.index(p) for p in range(phases)], jnp.int32)
            every = every[jnp.arange(vox) ^ me_vox][:, back_to[jnp.arange(phases) ^ me_phase]]
            pieces = [every.transpose(1, 0, 2, 3).reshape(spots, plans)]
        *outgoing, block_dose = forward(scalars, terms, pieces, rows, vox, masks)
        returned, dose = [], []
        for h in range(CHUNKS):
            if h > 0:
                outgoing = forward_later(h, scalars, terms[2], block_dose, give, vox)
            give, keep = place(which, received, exchange(outgoing), local_blocks)
            mine, other = phase_halves(give, keep)
            back = pull(which, received, mine, other, goals[h], scales[h], vox, last)
            returned += exchange(back[: vox // cores])
            dose += back[vox // cores :]
        parts = gradient_parts(scalars, terms, returned, rows, vox, masks)
        if rows % 8:
            parts = parts[0].reshape(phases, vox, rows, plans)
            wanted = jnp.asarray(masks, jnp.int32) ^ me_phase
            parts = parts[wanted][:, jnp.arange(vox) ^ me_vox]
            parts = parts.transpose(1, 0, 2, 3).reshape(vox // cores, cores, phases * rows, plans)
            parts = [parts[:, c] for c in range(cores)]
        total = sum_chips(parts)
        if last:
            split = total.reshape(phases, rows, plans)
            total = split[0]
            for i, m in enumerate(masks[1:], 1):
                total = total + swap(split[i], PHASE, m)
            new_weights = jnp.maximum(held[:rows] - step_size[None, :] * total, 0.0)
        else:
            total = sum_everywhere(total.reshape(phases, rows, plans), PHASE, phase_steps())
            held = jnp.maximum(held - step_size[None, :] * total.reshape(held.shape), 0.0)
    dose_field = jnp.stack(dose, axis=1).reshape(vox_rows, plans)
    return (new_weights, dose_field)


def solution(mesh):
    in_specs = (
        P("phase", "vox", None),
        P(("phase", "vox"), None),
        P(),
        P("phase", "vox", None),
        P("phase", "vox"),
        P("phase", "vox"),
        P("vox"),
        P(),
        P(),
        P(),
    )
    out_specs = (P(("phase", "vox"), None), P("vox", None))
    return jax.shard_map(
        per_device, mesh=mesh, in_specs=in_specs, out_specs=out_specs, check_vma=False
    )
```

```python
import functools

import jax
import jax.numpy as jnp
from jax import lax
from jax.experimental import pallas as pl
from jax.experimental.pallas import tpu as pltpu
from jax.sharding import PartitionSpec as P

CAP = 2
NSTRUCT = 8
ITERS = 2
CHUNKS = 2
VOX = "vox"
PHASE = "phase"
LABEL_ROWS = 16
F32 = jnp.float32
BF16 = jnp.bfloat16
LARGE = 14 << 20
SMALL = 4 << 20
ROWS_AT_ONCE = 1024
COLUMNS_AT_ONCE = 512
HUGE = 36 << 20
BRIEF = pl.CostEstimate(flops=1, bytes_accessed=1, transcendentals=0)


def swap(x, axis, mask):
    count = lax.axis_size(axis)
    return lax.ppermute(x, axis, [(i, i ^ mask) for i in range(count)])


def spread(x, axis, masks):
    return [x] + [swap(x, axis, m) for m in masks]


def core_count():
    return min(2, lax.axis_size(VOX))


def halves(x, axis):
    big = x.astype(BF16)
    small = (x - big.astype(F32)).astype(BF16)
    return jnp.concatenate([big, small], axis=axis)


def term_sum(full, rows, cols):
    return full[:rows, :cols] + (full[:rows, cols:] + full[rows:, :cols])


def specs(count, space):
    return [pl.BlockSpec(memory_space=space)] * count


def fill_weights(me_ref, out, pieces, rows, vox, masks):
    cores = len(pieces)
    for c, ref in enumerate(pieces):
        for k in range(vox // cores):
            for i, p in enumerate(masks):
                v = me_ref[0] ^ (k * cores + c)
                at = ((me_ref[1] ^ p) * vox + v) * rows
                out[pl.ds(pl.multiple_of(at, rows), rows), :] = halves(
                    ref[k, i * rows : (i + 1) * rows, :], 1
                )


def warp_chunk(h, chunks, cores, source_ref, valid_ref, tiles, dose, outs):
    height = tiles.shape[1]
    part = height // chunks
    for c, out in enumerate(outs):
        for k in range(out.shape[0]):
            for j in range(CAP):
                s = (k * cores + c) * CAP + j
                b = source_ref[s]
                block = dose[pl.ds(pl.multiple_of(b * height, height), height), :]
                tile = tiles[b, h * part : (h + 1) * part, :]
                left = jnp.concatenate([tile[:, :height], tile[:, height:]], axis=0)
                full = jnp.dot(left, halves(block, 1), preferred_element_type=F32)
                warped = term_sum(full, part, dose.shape[1])
                out[k, j] = jnp.where(valid_ref[s] > 0, warped, 0.0)


def forward_body(dims, source_ref, valid_ref, me_ref, big, small, tiles, *refs):
    vox, masks, rows, pieces_n, chunks, cores = dims
    pieces, outs = refs[:pieces_n], refs[pieces_n:-2]
    dose, weights = refs[-2:]
    plans = dose.shape[1]
    if len(pieces[0].shape) == 2:
        weights[...] = halves(pieces[0][...], 1)
    else:
        fill_weights(me_ref, weights, pieces, rows, vox, masks)
    step = min(ROWS_AT_ONCE, dose.shape[0])
    for first in range(0, dose.shape[0], step):
        at = slice(first, first + step)
        top = jnp.dot(big[at, :], weights[...], preferred_element_type=F32)
        rest = jnp.dot(small[at, :], weights[:, :plans], preferred_element_type=F32)
        dose[at, :] = top[:, :plans] + (top[:, plans:] + rest)
    warp_chunk(0, chunks, cores, source_ref, valid_ref, tiles, dose, outs)


def first_body(
    dims, source_ref, valid_ref, me_ref, tile_ref, matrix, warp_tiles, *refs
):
    vox, masks, rows, pieces_n, chunks, cores = dims
    pieces, outs = refs[:pieces_n], refs[pieces_n:-9]
    dose, big, small, tiles, weights, buffer, tile_buffer, sems, tile_sems = refs[-9:]
    plans = dose.shape[1]
    steps, height = buffer.shape[:2]
    count = tiles.shape[0]

    def fetch(i):
        return pltpu.make_async_copy(
            matrix.at[pl.ds(i * height, height)], buffer.at[i], sems.at[i]
        )

    def fetch_tile(b):
        return pltpu.make_async_copy(warp_tiles.at[tile_ref[b]], tile_buffer.at[b], tile_sems.at[b])

    def multiply(i):
        at = slice(i * height, (i + 1) * height)
        top = jnp.dot(big[at, :], weights[...], preferred_element_type=F32)
        rest = jnp.dot(small[at, :], weights[:, :plans], preferred_element_type=F32)
        dose[at, :] = top[:, :plans] + (top[:, plans:] + rest)

    for i in range(steps):
        fetch(i).start()
    for b in range(count):
        fetch_tile(b).start()
    if len(pieces[0].shape) == 2:
        weights[...] = halves(pieces[0][...], 1)
    else:
        fill_weights(me_ref, weights, pieces, rows, vox, masks)
    for i in range(steps):
        fetch(i).wait()
        x = buffer[i]
        top = x.astype(BF16)
        big[i * height : (i + 1) * height, :] = top
        small[i * height : (i + 1) * height, :] = (x - top.astype(F32)).astype(BF16)
        if i > 0:
            multiply(i - 1)
    for b in range(count):
        fetch_tile(b).wait()
        tiles[b] = halves(tile_buffer[b], 1)
    multiply(steps - 1)
    warp_chunk(0, chunks, cores, source_ref, valid_ref, tiles, dose, outs)


def first_forward(scalars, tile_index, matrix, warp_tiles, pieces, rows, vox, masks):
    height, width = warp_tiles.shape[1:]
    vox_rows, spots = matrix.shape
    plans = pieces[0].shape[-1]
    cores = core_count()
    count = vox_rows // height
    step = 2 * height
    out = jax.ShapeDtypeStruct((vox // cores, CAP, height // CHUNKS, plans), F32)
    terms = jax.ShapeDtypeStruct(matrix.shape, BF16)
    outs = [out] * cores + [
        jax.ShapeDtypeStruct((vox_rows, plans), F32),
        terms,
        terms,
        jax.ShapeDtypeStruct((count, height, 2 * width), BF16),
    ]
    return pl.pallas_call(
        functools.partial(first_body, (vox, masks, rows, len(pieces), CHUNKS, cores)),
        in_specs=specs(4, pltpu.SMEM) + specs(2, pltpu.HBM) + specs(len(pieces), pltpu.VMEM),
        out_specs=specs(len(outs), pltpu.VMEM),
        out_shape=outs,
        scratch_shapes=[
            pltpu.VMEM((spots, 2 * plans), BF16),
            pltpu.VMEM((vox_rows // step, step, spots), F32),
            pltpu.VMEM((count, height, width), F32),
            pltpu.SemaphoreType.DMA((vox_rows // step,)),
            pltpu.SemaphoreType.DMA((count,)),
        ],
        compiler_params=pltpu.CompilerParams(vmem_limit_bytes=HUGE),
        cost_estimate=BRIEF,
        name="first_dose_and_warp",
    )(*scalars, tile_index, matrix, warp_tiles, *pieces)


def forward(scalars, terms, pieces, rows, vox, masks):
    big, small, tiles = terms
    height = tiles.shape[1]
    vox_rows, spots = big.shape
    plans = pieces[0].shape[-1]
    cores = core_count()
    out = jax.ShapeDtypeStruct((vox // cores, CAP, height // CHUNKS, plans), F32)
    outs = [out] * cores + [jax.ShapeDtypeStruct((vox_rows, plans), F32)]
    return pl.pallas_call(
        functools.partial(forward_body, (vox, masks, rows, len(pieces), CHUNKS, cores)),
        in_specs=specs(3, pltpu.SMEM) + specs(3 + len(pieces), pltpu.VMEM),
        out_specs=specs(len(outs), pltpu.VMEM),
        out_shape=outs,
        scratch_shapes=[pltpu.VMEM((spots, 2 * plans), BF16)],
        compiler_params=pltpu.CompilerParams(vmem_limit_bytes=LARGE),
        cost_estimate=BRIEF,
        name="dose_and_warp",
    )(*scalars, *terms, *pieces)


def later_body(h, chunks, cores, source_ref, valid_ref, tiles, dose, after, *outs):
    warp_chunk(h, chunks, cores, source_ref, valid_ref, tiles, dose, outs)


def forward_later(h, scalars, tiles, dose, after, vox):
    height = tiles.shape[1]
    cores = core_count()
    out = jax.ShapeDtypeStruct((vox // cores, CAP, height // CHUNKS, dose.shape[1]), F32)
    return pl.pallas_call(
        functools.partial(later_body, h, CHUNKS, cores),
        in_specs=specs(2, pltpu.SMEM) + specs(2, pltpu.VMEM) + specs(1, pl.ANY),
        out_specs=specs(cores, pltpu.VMEM),
        out_shape=[out] * cores,
        compiler_params=pltpu.CompilerParams(vmem_limit_bytes=SMALL),
        cost_estimate=BRIEF,
        name="warp_later",
    )(*scalars[:2], tiles, dose, after)


def piece(arrived, cores, m):
    return arrived[m // cores].at[m % cores]


def gradient_body(dims, source_ref, valid_ref, me_ref, big, small, tiles, *refs):
    vox, masks, rows, cores, chunks = dims
    chips = vox // cores
    returned = refs[: chips * chunks]
    outs = refs[chips * chunks : -2]
    columns, turned = refs[-2:]
    height = tiles.shape[1]
    plans = turned.shape[1]
    vox_rows, spots = big.shape
    spare = vox_rows // height
    for m in range(vox):
        found = [piece(returned[h * chips : (h + 1) * chips], cores, m) for h in range(chunks)]
        for j in range(CAP):
            s = m * CAP + j
            b = source_ref[s]
            adjoint = jnp.concatenate([f[j] for f in found], axis=0)
            full = jnp.dot(halves(adjoint.T, 0), tiles[b], preferred_element_type=F32)
            to = jnp.where(valid_ref[s] > 0, b, spare) * height
            columns[:, pl.ds(pl.multiple_of(to, height), height)] = halves(
                term_sum(full, plans, height), 0
            )

    for first in range(0, spots, COLUMNS_AT_ONCE):
        last = min(first + COLUMNS_AT_ONCE, spots)
        top = jnp.dot(columns[:, :vox_rows], big[:, first:last], preferred_element_type=F32)
        rest = jnp.dot(
            columns[:plans, :vox_rows], small[:, first:last], preferred_element_type=F32
        )
        total = top[:plans] + (top[plans:] + rest)
        for i in range(0, last - first, plans):
            turned[first + i : first + i + plans, :] = total[:, i : i + plans].T
    if len(outs[0].shape) == 2:
        outs[0][...] = turned[...]
    else:
        for c in range(cores):
            for k in range(vox // cores):
                for i, p in enumerate(masks):
                    v = me_ref[0] ^ (k * cores + c)
                    at = ((me_ref[1] ^ p) * vox + v) * rows
                    outs[c][k, i * rows : (i + 1) * rows] = turned[
                        pl.ds(pl.multiple_of(at, rows), rows), :
                    ]


def gradient_parts(scalars, terms, returned, rows, vox, masks):
    big, small, tiles = terms
    vox_rows, spots = big.shape
    plans = returned[0].shape[-1]
    cores = core_count()
    if rows % 8 == 0:
        outs = [jax.ShapeDtypeStruct((vox // cores, len(masks) * rows, plans), F32)] * cores
    else:
        outs = [jax.ShapeDtypeStruct((spots, plans), F32)]
    return pl.pallas_call(
        functools.partial(gradient_body, (vox, masks, rows, cores, CHUNKS)),
        in_specs=specs(3, pltpu.SMEM) + specs(3 + len(returned), pltpu.VMEM),
        out_specs=specs(len(outs), pltpu.VMEM),
        out_shape=outs,
        scratch_shapes=[pltpu.VMEM((2 * plans, vox_rows + tiles.shape[1]), BF16),
            pltpu.VMEM((spots, plans), F32),
        ],
        compiler_params=pltpu.CompilerParams(vmem_limit_bytes=LARGE),
        cost_estimate=BRIEF,
        name="warp_back_and_gradient",
    )(*scalars, *terms, *returned)


def place_body(vox, cores, which_ref, slot_ref, *refs):
    chips = vox // cores
    arrived, (give, keep, total) = refs[:chips], refs[chips:]
    total[...] = jnp.zeros_like(total)
    for m in range(vox):
        blocks = piece(arrived, cores, m)
        for j in range(CAP):
            slot = slot_ref[m * CAP + j]

            @pl.when(slot >= 0)
            def _():
                total[slot] += blocks[j]

    half = keep.shape[0]
    which = which_ref[0]
    keep[...] = total[pl.ds(which * half, half)]
    give[...] = total[pl.ds((1 - which) * half, half)]


def place(which, slots, incoming, blocks):
    cores = core_count()
    vox = len(incoming) * cores
    height, plans = incoming[0].shape[-2:]
    half = jax.ShapeDtypeStruct((blocks // 2, height, plans), F32)
    return pl.pallas_call(
        functools.partial(place_body, vox, cores),
        in_specs=specs(2, pltpu.SMEM) + specs(len(incoming), pltpu.VMEM),
        out_specs=specs(2, pltpu.VMEM),
        out_shape=[half, half],
        scratch_shapes=[pltpu.VMEM((blocks, height, plans), F32)],
        compiler_params=pltpu.CompilerParams(vmem_limit_bytes=SMALL),
        cost_estimate=BRIEF,
        name="place_blocks",
    )(which, slots, *incoming)


def pull_body(vox, cores, with_dose, which_ref, slot_ref, mine, other, goal, scale, *refs):
    half = mine.shape[0]
    which = which_ref[0]
    field = refs[-1]
    field[pl.ds(which * half, half)] = mine[...]
    field[pl.ds((1 - which) * half, half)] = other[...]
    for m in range(vox):
        for j in range(CAP):
            slot = jnp.maximum(slot_ref[m * CAP + j], 0)
            refs[m % cores][m // cores, j] = scale[slot] * (field[slot] - goal[slot])
    if with_dose:
        refs[cores][...] = field[...]


def pull(which, slots, mine, other, goal, scale, vox, with_dose):
    half, height, plans = mine.shape
    cores = core_count()
    outs = [jax.ShapeDtypeStruct((vox // cores, CAP, height, plans), F32)] * cores
    if with_dose:
        outs = outs + [jax.ShapeDtypeStruct((2 * half, height, plans), F32)]
    return pl.pallas_call(
        functools.partial(pull_body, vox, cores, with_dose),
        in_specs=specs(2, pltpu.SMEM) + specs(4, pltpu.VMEM),
        out_specs=specs(len(outs), pltpu.VMEM),
        out_shape=outs,
        scratch_shapes=[pltpu.VMEM((2 * half, height, plans), F32)],
        compiler_params=pltpu.CompilerParams(vmem_limit_bytes=SMALL),
        cost_estimate=BRIEF,
        name="adjoint_blocks",
    )(which, slots, mine, other, goal, scale)


def phase_steps():
    count, steps = lax.axis_size(PHASE), []
    while 2 ** len(steps) < count:
        steps.append(2 ** (len(steps) + 1) - 1)
    return steps


def combined(steps):
    masks = [0]
    for s in steps:
        masks += [m ^ s for m in masks]
    return masks


def sum_everywhere(x, axis, steps):
    for i, s in enumerate(steps):
        other = swap(x, axis, s).reshape(-1, 2, 2**i, *x.shape[1:])
        x = x + jnp.concatenate([other[:, 1:], other[:, :1]], axis=1).reshape(x.shape)
    return x


def gather_chips(by_phase):
    cores = core_count()
    by_chip = jnp.stack(spread(by_phase, VOX, range(cores, lax.axis_size(VOX), cores)))
    return spread(by_chip, VOX, range(1, cores))


def sum_chips(parts):
    cores = len(parts)
    chips = parts[0]
    for m in range(1, cores):
        chips = chips + swap(parts[m], VOX, m)
    mine = chips[0]
    for k in range(1, chips.shape[0]):
        mine = mine + swap(chips[k], VOX, k * cores)
    return mine


def exchange(pieces):
    cores = len(pieces)
    crossed = [pieces[0]] + [swap(pieces[c], VOX, c) for c in range(1, cores)]
    chips = [jnp.stack([p[k] for p in crossed]) for k in range(pieces[0].shape[0])]
    return [chips[0]] + [swap(chips[k], VOX, k * cores) for k in range(1, len(chips))]


def phase_halves(give, keep):
    phases = lax.axis_size(PHASE)
    if phases == 1:
        return keep, give
    keep = keep + swap(give, PHASE, 1)
    span = 4
    while span <= phases:
        keep = keep + swap(keep, PHASE, span - 1)
        span *= 2
    return keep, swap(keep, PHASE, 1)


def per_device(
    influence,
    weights,
    warp_tiles,
    owners,
    owner_slot,
    tile_index,
    structure,
    prescribed,
    importance,
    step_size,
):
    highest = lax.Precision.HIGHEST
    matrix = influence[0]
    vox_rows, spots = matrix.shape
    block_rows = warp_tiles.shape[1]
    rows, plans = weights.shape
    local_blocks = vox_rows // block_rows
    vox = lax.axis_size(VOX)
    phases = lax.axis_size(PHASE)
    cores = core_count()
    me_vox = lax.axis_index(VOX)
    me_phase = lax.axis_index(PHASE)
    slots_all = vox * CAP
    part = block_rows // CHUNKS
    targets = owners[0, :, 0]
    which = ((me_phase ^ (me_phase >> 1)) & 1).astype(jnp.int32).reshape(1)

    def orders(names):
        before = jnp.tril(jnp.ones((local_blocks, local_blocks), jnp.int32), -1)
        same = (names[..., :, None] == names[..., None, :]).astype(jnp.int32)
        return jnp.sum(same * before, axis=-1)

    position = (targets ^ me_vox) * CAP + orders(targets)
    chosen_mask = jnp.arange(slots_all, dtype=jnp.int32)[:, None] == position[None, :]
    positions_i = jnp.arange(local_blocks, dtype=jnp.int32)
    source = jnp.sum(jnp.where(chosen_mask, positions_i[None, :], 0), axis=1)
    valid = jnp.sum(chosen_mask.astype(jnp.int32), axis=1)
    me = jnp.stack([me_vox, me_phase]).astype(jnp.int32)
    scalars = (source, valid, me)
    labels = jnp.zeros((LABEL_ROWS, plans), F32)
    labels = labels.at[0, :local_blocks].set(targets.astype(F32))
    labels = labels.at[1, :local_blocks].set(owner_slot[0].astype(F32))

    member = (structure[:, None] == jnp.arange(NSTRUCT, dtype=jnp.int32)[None, :]).astype(F32)
    target_dose = jnp.dot(member, prescribed, precision=highest, preferred_element_type=F32)
    voxel_weight = jnp.dot(
        member, importance[:, None], precision=highest, preferred_element_type=F32
    )
    voxel_weight = jnp.broadcast_to(voxel_weight, target_dose.shape)
    goals = target_dose.reshape(local_blocks, CHUNKS, part, plans)
    scales = voxel_weight.reshape(local_blocks, CHUNKS, part, plans)
    goals = [goals[:, h] for h in range(CHUNKS)]
    scales = [scales[:, h] for h in range(CHUNKS)]

    masks = combined(phase_steps())
    held = jnp.concatenate(spread(weights, PHASE, masks[1:]), axis=0)
    for iteration in range(ITERS):
        last = iteration == ITERS - 1
        if iteration == 0:
            pieces = gather_chips(jnp.concatenate([held, labels], axis=0))
            infos = jnp.stack(pieces, axis=1).reshape(vox, -1, plans)[:, phases * rows :]
            names = infos[:, 0, :local_blocks].astype(jnp.int32)
            slots = infos[:, 1, :local_blocks].astype(jnp.int32)
            order = jnp.where(names == me_vox, orders(names), -1)
            hit = order[:, None, :] == jnp.arange(CAP, dtype=jnp.int32)[None, :, None]
            received = jnp.sum(jnp.where(hit, slots[:, None, :] + 1, 0), axis=-1)
            received = received.reshape(slots_all) - 1
        else:
            pieces = gather_chips(held)
        if rows % 16:
            every = jnp.stack(pieces, axis=1).reshape(vox, -1, plans)[:, : phases * rows]
            every = every.reshape(vox, phases, rows, plans)
            back_to = jnp.asarray([masks.index(p) for p in range(phases)], jnp.int32)
            every = every[jnp.arange(vox) ^ me_vox][:, back_to[jnp.arange(phases) ^ me_phase]]
            pieces = [every.transpose(1, 0, 2, 3).reshape(spots, plans)]
        if iteration == 0:
            *outgoing, block_dose, big, small, own_tiles = first_forward(
                scalars, tile_index[0], matrix, warp_tiles, pieces, rows, vox, masks
            )
            terms = (big, small, own_tiles)
        else:
            *outgoing, block_dose = forward(scalars, terms, pieces, rows, vox, masks)
        returned, dose = [], []
        for h in range(CHUNKS):
            if h > 0:
                outgoing = forward_later(h, scalars, terms[2], block_dose, give, vox)
            give, keep = place(which, received, exchange(outgoing), local_blocks)
            mine, other = phase_halves(give, keep)
            back = pull(which, received, mine, other, goals[h], scales[h], vox, last)
            returned += exchange(back[:cores])
            dose += back[cores:]
        parts = gradient_parts(scalars, terms, returned, rows, vox, masks)
        if rows % 8:
            parts = parts[0].reshape(phases, vox, rows, plans)
            wanted = jnp.asarray(masks, jnp.int32) ^ me_phase
            parts = parts[wanted][:, jnp.arange(vox) ^ me_vox]
            parts = parts.transpose(1, 0, 2, 3).reshape(vox // cores, cores, phases * rows, plans)
            parts = [parts[:, c] for c in range(cores)]
        total = sum_chips(parts)
        if last:
            split = total.reshape(phases, rows, plans)
            total = split[0]
            for i, m in enumerate(masks[1:], 1):
                total = total + swap(split[i], PHASE, m)
            new_weights = jnp.maximum(held[:rows] - step_size[None, :] * total, 0.0)
        else:
            total = sum_everywhere(total.reshape(phases, rows, plans), PHASE, phase_steps())
            held = jnp.maximum(held - step_size[None, :] * total.reshape(held.shape), 0.0)
    dose_field = jnp.stack(dose, axis=1).reshape(vox_rows, plans)
    return (new_weights, dose_field)


def solution(mesh):
    in_specs = (
        P("phase", "vox", None),
        P(("phase", "vox"), None),
        P(),
        P("phase", "vox", None),
        P("phase", "vox"),
        P("phase", "vox"),
        P("vox"),
        P(),
        P(),
        P(),
    )
    out_specs = (P(("phase", "vox"), None), P("vox", None))
    return jax.shard_map(
        per_device, mesh=mesh, in_specs=in_specs, out_specs=out_specs, check_vma=False
    )
```

```python
import functools

import jax
import jax.numpy as jnp
from jax import lax
from jax.experimental import pallas as pl
from jax.experimental.pallas import tpu as pltpu
from jax.sharding import PartitionSpec as P

CAP = 2
NSTRUCT = 8
ITERS = 2
CHUNKS = 2
VOX = "vox"
PHASE = "phase"
LABEL_ROWS = 16
F32 = jnp.float32
BF16 = jnp.bfloat16
LARGE = 14 << 20
SMALL = 4 << 20
ROWS_AT_ONCE = 512
BLOCK_ROWS_AT_ONCE = 256
BRIEF = pl.CostEstimate(flops=1, bytes_accessed=1, transcendentals=0)


def swap(x, axis, mask):
    count = lax.axis_size(axis)
    return lax.ppermute(x, axis, [(i, i ^ mask) for i in range(count)])


def spread(x, axis, masks):
    return [x] + [swap(x, axis, m) for m in masks]


def core_count():
    return min(2, lax.axis_size(VOX))


def terms(x):
    big = x.astype(BF16)
    return big, (x - big.astype(F32)).astype(BF16)


def halves(x, axis):
    return jnp.concatenate(terms(x), axis=axis)


def term_sum(full, rows, cols):
    return full[:rows, :cols] + (full[:rows, cols:] + full[rows:, :cols])


def specs(count, space):
    return [pl.BlockSpec(memory_space=space)] * count


def fill_weights(me_ref, out, pieces, rows, vox, masks):
    cores = len(pieces)
    for c, ref in enumerate(pieces):
        for k in range(vox // cores):
            for i, p in enumerate(masks):
                v = me_ref[0] ^ (k * cores + c)
                at = ((me_ref[1] ^ p) * vox + v) * rows
                out[pl.ds(pl.multiple_of(at, rows), rows), :] = halves(
                    ref[k, i * rows : (i + 1) * rows, :], 1
                )


def warp(chunks, cores, source_ref, valid_ref, tiles, dose, outs):
    height = tiles.shape[1]
    plans = dose.shape[1]
    part = height // chunks
    for c in range(cores):
        for k in range(outs[0].shape[0]):
            for j in range(CAP):
                s = (k * cores + c) * CAP + j
                b = source_ref[s]
                block = dose[pl.ds(pl.multiple_of(b * height, height), height), :]
                full = jnp.dot(
                    halves(tiles[b], 0), halves(block, 1), preferred_element_type=F32
                )
                warped = jnp.where(valid_ref[s] > 0, term_sum(full, height, plans), 0.0)
                for h in range(chunks):
                    outs[h * cores + c][k, j] = warped[h * part : (h + 1) * part]


def forward_body(dims, source_ref, valid_ref, me_ref, matrix, tiles, *refs):
    vox, masks, rows, pieces_n, chunks, cores = dims
    pieces, outs = refs[:pieces_n], refs[pieces_n:-2]
    dose, weights = refs[-2:]
    plans = dose.shape[1]
    if len(pieces[0].shape) == 2:
        weights[...] = halves(pieces[0][...], 1)
    else:
        fill_weights(me_ref, weights, pieces, rows, vox, masks)
    step = min(ROWS_AT_ONCE, dose.shape[0])
    for first in range(0, dose.shape[0], step):
        at = slice(first, first + step)
        big, small = terms(matrix[at, :])
        top = jnp.dot(big, weights[...], preferred_element_type=F32)
        rest = jnp.dot(small, weights[:, :plans], preferred_element_type=F32)
        dose[at, :] = top[:, :plans] + (top[:, plans:] + rest)
    warp(chunks, cores, source_ref, valid_ref, tiles, dose, outs)


def forward(scalars, matrix, tiles, pieces, rows, vox, masks):
    height = tiles.shape[1]
    vox_rows, spots = matrix.shape
    plans = pieces[0].shape[-1]
    cores = core_count()
    out = jax.ShapeDtypeStruct((vox // cores, CAP, height // CHUNKS, plans), F32)
    outs = [out] * (cores * CHUNKS)
    return pl.pallas_call(
        functools.partial(forward_body, (vox, masks, rows, len(pieces), CHUNKS, cores)),
        in_specs=specs(3, pltpu.SMEM) + specs(2 + len(pieces), pltpu.VMEM),
        out_specs=specs(len(outs), pltpu.VMEM),
        out_shape=outs,
        scratch_shapes=[pltpu.VMEM((vox_rows, plans), F32), pltpu.VMEM((spots, 2 * plans), BF16)],
        compiler_params=pltpu.CompilerParams(vmem_limit_bytes=LARGE),
        cost_estimate=BRIEF,
        name="dose_and_warp",
    )(*scalars, matrix, tiles, *pieces)


def piece(arrived, cores, m):
    return arrived[m // cores].at[m % cores]


def gradient_body(dims, source_ref, valid_ref, me_ref, matrix, tiles, *refs):
    vox, masks, rows, cores, chunks = dims
    chips = vox // cores
    returned = refs[: chips * chunks]
    outs = refs[chips * chunks : -3]
    columns, total, turned = refs[-3:]
    height = tiles.shape[1]
    plans = turned.shape[1]
    vox_rows, spots = matrix.shape
    spare = vox_rows // height
    for m in range(vox):
        found = [piece(returned[h * chips : (h + 1) * chips], cores, m) for h in range(chunks)]
        for j in range(CAP):
            s = m * CAP + j
            b = source_ref[s]
            adjoint = jnp.concatenate([f[j] for f in found], axis=0)
            full = jnp.dot(
                halves(adjoint.T, 0), halves(tiles[b], 1), preferred_element_type=F32
            )
            to = jnp.where(valid_ref[s] > 0, b, spare) * height
            columns[:, pl.ds(pl.multiple_of(to, height), height)] = halves(
                term_sum(full, plans, height), 0
            )

    step = min(BLOCK_ROWS_AT_ONCE, vox_rows)
    for first in range(0, vox_rows, step):
        at = slice(first, first + step)
        big, small = terms(matrix[at, :])
        top = jnp.dot(columns[:, at], big, preferred_element_type=F32)
        rest = jnp.dot(columns[:plans, at], small, preferred_element_type=F32)
        part = top[:plans] + (top[plans:] + rest)
        total[...] = part if first == 0 else total[...] + part
    for i in range(0, spots, plans):
        turned[i : i + plans, :] = total[:, i : i + plans].T
    if len(outs[0].shape) == 2:
        outs[0][...] = turned[...]
    else:
        for c in range(cores):
            for k in range(vox // cores):
                for i, p in enumerate(masks):
                    v = me_ref[0] ^ (k * cores + c)
                    at = ((me_ref[1] ^ p) * vox + v) * rows
                    outs[c][k, i * rows : (i + 1) * rows] = turned[
                        pl.ds(pl.multiple_of(at, rows), rows), :
                    ]


def gradient_parts(scalars, matrix, tiles, returned, rows, vox, masks):
    vox_rows, spots = matrix.shape
    plans = returned[0].shape[-1]
    cores = core_count()
    if rows % 8 == 0:
        outs = [jax.ShapeDtypeStruct((vox // cores, len(masks) * rows, plans), F32)] * cores
    else:
        outs = [jax.ShapeDtypeStruct((spots, plans), F32)]
    return pl.pallas_call(
        functools.partial(gradient_body, (vox, masks, rows, cores, CHUNKS)),
        in_specs=specs(3, pltpu.SMEM) + specs(2 + len(returned), pltpu.VMEM),
        out_specs=specs(len(outs), pltpu.VMEM),
        out_shape=outs,
        scratch_shapes=[pltpu.VMEM((2 * plans, vox_rows + tiles.shape[1]), BF16),
            pltpu.VMEM((plans, spots), F32),
            pltpu.VMEM((spots, plans), F32),
        ],
        compiler_params=pltpu.CompilerParams(vmem_limit_bytes=LARGE),
        cost_estimate=BRIEF,
        name="warp_back_and_gradient",
    )(*scalars, matrix, tiles, *returned)


def place_body(vox, cores, which_ref, slot_ref, *refs):
    chips = vox // cores
    arrived, (give, keep, total) = refs[:chips], refs[chips:]
    total[...] = jnp.zeros_like(total)
    for m in range(vox):
        blocks = piece(arrived, cores, m)
        for j in range(CAP):
            slot = slot_ref[m * CAP + j]

            @pl.when(slot >= 0)
            def _():
                total[slot] += blocks[j]

    half = keep.shape[0]
    which = which_ref[0]
    keep[...] = total[pl.ds(which * half, half)]
    give[...] = total[pl.ds((1 - which) * half, half)]


def place(which, slots, incoming, blocks):
    cores = core_count()
    vox = len(incoming) * cores
    height, plans = incoming[0].shape[-2:]
    half = jax.ShapeDtypeStruct((blocks // 2, height, plans), F32)
    return pl.pallas_call(
        functools.partial(place_body, vox, cores),
        in_specs=specs(2, pltpu.SMEM) + specs(len(incoming), pltpu.VMEM),
        out_specs=specs(2, pltpu.VMEM),
        out_shape=[half, half],
        scratch_shapes=[pltpu.VMEM((blocks, height, plans), F32)],
        compiler_params=pltpu.CompilerParams(vmem_limit_bytes=SMALL),
        cost_estimate=BRIEF,
        name="place_blocks",
    )(which, slots, *incoming)


def pull_body(vox, cores, with_dose, which_ref, slot_ref, mine, other, goal, scale, *refs):
    half = mine.shape[0]
    which = which_ref[0]
    field = refs[-1]
    field[pl.ds(which * half, half)] = mine[...]
    field[pl.ds((1 - which) * half, half)] = other[...]
    for m in range(vox):
        for j in range(CAP):
            slot = jnp.maximum(slot_ref[m * CAP + j], 0)
            refs[m % cores][m // cores, j] = scale[slot] * (field[slot] - goal[slot])
    if with_dose:
        refs[cores][...] = field[...]


def pull(which, slots, mine, other, goal, scale, vox, with_dose):
    half, height, plans = mine.shape
    cores = core_count()
    outs = [jax.ShapeDtypeStruct((vox // cores, CAP, height, plans), F32)] * cores
    if with_dose:
        outs = outs + [jax.ShapeDtypeStruct((2 * half, height, plans), F32)]
    return pl.pallas_call(
        functools.partial(pull_body, vox, cores, with_dose),
        in_specs=specs(2, pltpu.SMEM) + specs(4, pltpu.VMEM),
        out_specs=specs(len(outs), pltpu.VMEM),
        out_shape=outs,
        scratch_shapes=[pltpu.VMEM((2 * half, height, plans), F32)],
        compiler_params=pltpu.CompilerParams(vmem_limit_bytes=SMALL),
        cost_estimate=BRIEF,
        name="adjoint_blocks",
    )(which, slots, mine, other, goal, scale)


def phase_steps():
    count, steps = lax.axis_size(PHASE), []
    while 2 ** len(steps) < count:
        steps.append(2 ** (len(steps) + 1) - 1)
    return steps


def combined(steps):
    masks = [0]
    for s in steps:
        masks += [m ^ s for m in masks]
    return masks


def sum_everywhere(x, axis, steps):
    for i, s in enumerate(steps):
        other = swap(x, axis, s).reshape(-1, 2, 2**i, *x.shape[1:])
        x = x + jnp.concatenate([other[:, 1:], other[:, :1]], axis=1).reshape(x.shape)
    return x


def gather_chips(by_phase):
    cores = core_count()
    by_chip = jnp.stack(spread(by_phase, VOX, range(cores, lax.axis_size(VOX), cores)))
    return spread(by_chip, VOX, range(1, cores))


def sum_chips(parts):
    cores = len(parts)
    chips = parts[0]
    for m in range(1, cores):
        chips = chips + swap(parts[m], VOX, m)
    mine = chips[0]
    for k in range(1, chips.shape[0]):
        mine = mine + swap(chips[k], VOX, k * cores)
    return mine


def cross(pieces):
    cores = len(pieces)
    crossed = [pieces[0]] + [swap(pieces[c], VOX, c) for c in range(1, cores)]
    return [jnp.stack([p[k] for p in crossed]) for k in range(pieces[0].shape[0])]


def send(chips):
    cores = core_count()
    return [chips[0]] + [swap(chips[k], VOX, k * cores) for k in range(1, len(chips))]


def exchange(pieces):
    return send(cross(pieces))


def phase_stages(half):
    for step in phase_steps()[1:-1]:
        half = half + swap(half, PHASE, step)
    return half, swap(half, PHASE, phase_steps()[-1])


def tie(x, other):
    return lax.optimization_barrier((x, other))[0]


def goals_and_scales(structure, prescribed, importance, blocks, height):
    highest = lax.Precision.HIGHEST
    member = (structure[:, None] == jnp.arange(NSTRUCT, dtype=jnp.int32)[None, :]).astype(F32)
    target_dose = jnp.dot(member, prescribed, precision=highest, preferred_element_type=F32)
    voxel_weight = jnp.dot(
        member, importance[:, None], precision=highest, preferred_element_type=F32
    )
    voxel_weight = jnp.broadcast_to(voxel_weight, target_dose.shape)
    shape = (blocks, CHUNKS, height // CHUNKS, prescribed.shape[1])
    cut = [x.reshape(shape) for x in (target_dose, voxel_weight)]
    return [[x[:, h] for h in range(CHUNKS)] for x in cut]


def per_device(
    influence,
    weights,
    warp_tiles,
    owners,
    owner_slot,
    tile_index,
    structure,
    prescribed,
    importance,
    step_size,
):
    matrix = influence[0]
    vox_rows, spots = matrix.shape
    block_rows = warp_tiles.shape[1]
    rows, plans = weights.shape
    local_blocks = vox_rows // block_rows
    vox = lax.axis_size(VOX)
    phases = lax.axis_size(PHASE)
    cores = core_count()
    me_vox = lax.axis_index(VOX)
    me_phase = lax.axis_index(PHASE)
    slots_all = vox * CAP
    targets = owners[0, :, 0]
    which = ((me_phase ^ (me_phase >> 1)) & 1).astype(jnp.int32).reshape(1)

    def orders(names):
        before = jnp.tril(jnp.ones((local_blocks, local_blocks), jnp.int32), -1)
        same = (names[..., :, None] == names[..., None, :]).astype(jnp.int32)
        return jnp.sum(same * before, axis=-1)

    position = (targets ^ me_vox) * CAP + orders(targets)
    chosen_mask = jnp.arange(slots_all, dtype=jnp.int32)[:, None] == position[None, :]
    positions_i = jnp.arange(local_blocks, dtype=jnp.int32)
    source = jnp.sum(jnp.where(chosen_mask, positions_i[None, :], 0), axis=1)
    valid = jnp.sum(chosen_mask.astype(jnp.int32), axis=1)
    me = jnp.stack([me_vox, me_phase]).astype(jnp.int32)
    scalars = (source, valid, me)
    labels = jnp.zeros((LABEL_ROWS, plans), F32)
    labels = labels.at[0, :local_blocks].set(targets.astype(F32))
    labels = labels.at[1, :local_blocks].set(owner_slot[0].astype(F32))

    masks = combined(phase_steps())
    tiles = warp_tiles[tile_index[0]]
    held = jnp.concatenate(spread(weights, PHASE, masks[1:]), axis=0)
    for iteration in range(ITERS):
        last = iteration == ITERS - 1
        if iteration == 0:
            pieces = gather_chips(jnp.concatenate([held, labels], axis=0))
            infos = jnp.stack(pieces, axis=1).reshape(vox, -1, plans)[:, phases * rows :]
            names = infos[:, 0, :local_blocks].astype(jnp.int32)
            slots = infos[:, 1, :local_blocks].astype(jnp.int32)
            order = jnp.where(names == me_vox, orders(names), -1)
            hit = order[:, None, :] == jnp.arange(CAP, dtype=jnp.int32)[None, :, None]
            received = jnp.sum(jnp.where(hit, slots[:, None, :] + 1, 0), axis=-1)
            received = received.reshape(slots_all) - 1
        else:
            pieces = gather_chips(held)
        if rows % 16:
            every = jnp.stack(pieces, axis=1).reshape(vox, -1, plans)[:, : phases * rows]
            every = every.reshape(vox, phases, rows, plans)
            back_to = jnp.asarray([masks.index(p) for p in range(phases)], jnp.int32)
            every = every[jnp.arange(vox) ^ me_vox][:, back_to[jnp.arange(phases) ^ me_phase]]
            pieces = [every.transpose(1, 0, 2, 3).reshape(spots, plans)]
        outgoing = forward(scalars, matrix, tiles, pieces, rows, vox, masks)
        returned, dose = [], []
        incoming, held_halves, seconds = exchange(outgoing[:cores]), [], []
        for h in range(CHUNKS):
            give, keep = place(which, received, incoming, local_blocks)
            got = swap(give, PHASE, 1)
            if iteration == 0 and h == 0:
                goals, scales = goals_and_scales(
                    tie(structure, give), prescribed, importance, local_blocks, block_rows
                )
            if h + 1 < CHUNKS:
                later = outgoing[(h + 1) * cores : (h + 2) * cores]
                incoming = exchange([tie(x, incoming[1]) for x in later])
            if h > 0:
                got = tie(got, seconds[-1])
            half, second = phase_stages(keep + got)
            held_halves.append(half)
            seconds.append(second)
        for h in range(CHUNKS):
            second = seconds[h] if h == 0 else tie(seconds[h], other)
            mine = held_halves[h] + second
            other = swap(mine, PHASE, 1)
            back = pull(which, received, mine, other, goals[h], scales[h], vox, last)
            returned += exchange(back[:cores])
            dose += back[cores:]
        parts = gradient_parts(scalars, matrix, tiles, returned, rows, vox, masks)
        if rows % 8:
            parts = parts[0].reshape(phases, vox, rows, plans)
            wanted = jnp.asarray(masks, jnp.int32) ^ me_phase
            parts = parts[wanted][:, jnp.arange(vox) ^ me_vox]
            parts = parts.transpose(1, 0, 2, 3).reshape(vox // cores, cores, phases * rows, plans)
            parts = [parts[:, c] for c in range(cores)]
        total = sum_chips(parts)
        if last:
            split = total.reshape(phases, rows, plans)
            total = split[0]
            for i, m in enumerate(masks[1:], 1):
                total = total + swap(split[i], PHASE, m)
            new_weights = jnp.maximum(held[:rows] - step_size[None, :] * total, 0.0)
        else:
            total = sum_everywhere(total.reshape(phases, rows, plans), PHASE, phase_steps())
            held = jnp.maximum(held - step_size[None, :] * total.reshape(held.shape), 0.0)
    dose_field = jnp.stack(dose, axis=1).reshape(vox_rows, plans)
    return (new_weights, dose_field)


def solution(mesh):
    in_specs = (
        P("phase", "vox", None),
        P(("phase", "vox"), None),
        P(),
        P("phase", "vox", None),
        P("phase", "vox"),
        P("phase", "vox"),
        P("vox"),
        P(),
        P(),
        P(),
    )
    out_specs = (P(("phase", "vox"), None), P("vox", None))
    return jax.shard_map(
        per_device, mesh=mesh, in_specs=in_specs, out_specs=out_specs, check_vma=False
    )
```

```python
import functools

import jax
import jax.numpy as jnp
from jax import lax
from jax.experimental import pallas as pl
from jax.experimental.pallas import tpu as pltpu
from jax.sharding import PartitionSpec as P

CAP = 2
NSTRUCT = 8
ITERS = 2
CHUNKS = 2
VOX = "vox"
PHASE = "phase"
LABEL_ROWS = 16
F32 = jnp.float32
BF16 = jnp.bfloat16
LARGE = 14 << 20
SMALL = 4 << 20
ROWS_AT_ONCE = 512
BLOCK_ROWS_AT_ONCE = 256
BRIEF = pl.CostEstimate(flops=1, bytes_accessed=1, transcendentals=0)


def swap(x, axis, mask):
    count = lax.axis_size(axis)
    return lax.ppermute(x, axis, [(i, i ^ mask) for i in range(count)])


def spread(x, axis, masks):
    return [x] + [swap(x, axis, m) for m in masks]


def core_count():
    return min(2, lax.axis_size(VOX))


def terms(x):
    big = x.astype(BF16)
    return big, (x - big.astype(F32)).astype(BF16)


def halves(x, axis):
    return jnp.concatenate(terms(x), axis=axis)


def term_sum(full, rows, cols):
    return full[:rows, :cols] + (full[:rows, cols:] + full[rows:, :cols])


def specs(count, space):
    return [pl.BlockSpec(memory_space=space)] * count


def fill_weights(me_ref, out, pieces, rows, vox, masks):
    cores = len(pieces)
    for c, ref in enumerate(pieces):
        for k in range(vox // cores):
            for i, p in enumerate(masks):
                v = me_ref[0] ^ (k * cores + c)
                at = ((me_ref[1] ^ p) * vox + v) * rows
                out[pl.ds(pl.multiple_of(at, rows), rows), :] = halves(
                    ref[k, i * rows : (i + 1) * rows, :], 1
                )


def warp(chunks, cores, source_ref, valid_ref, tiles, dose, outs):
    height = tiles.shape[1]
    plans = dose.shape[1]
    part = height // chunks
    for c in range(cores):
        for k in range(outs[0].shape[0]):
            for j in range(CAP):
                s = (k * cores + c) * CAP + j
                b = source_ref[s]
                block = dose[pl.ds(pl.multiple_of(b * height, height), height), :]
                full = jnp.dot(
                    halves(tiles[b], 0), halves(block, 1), preferred_element_type=F32
                )
                warped = jnp.where(valid_ref[s] > 0, term_sum(full, height, plans), 0.0)
                for h in range(chunks):
                    outs[h * cores + c][k, j] = warped[h * part : (h + 1) * part]


def forward_body(dims, source_ref, valid_ref, me_ref, matrix, tiles, *refs):
    vox, masks, rows, pieces_n, chunks, cores = dims
    pieces, outs = refs[:pieces_n], refs[pieces_n:-2]
    dose, weights = refs[-2:]
    plans = dose.shape[1]
    if len(pieces[0].shape) == 2:
        weights[...] = halves(pieces[0][...], 1)
    else:
        fill_weights(me_ref, weights, pieces, rows, vox, masks)
    step = min(ROWS_AT_ONCE, dose.shape[0])
    for first in range(0, dose.shape[0], step):
        at = slice(first, first + step)
        big, small = terms(matrix[at, :])
        top = jnp.dot(big, weights[...], preferred_element_type=F32)
        rest = jnp.dot(small, weights[:, :plans], preferred_element_type=F32)
        dose[at, :] = top[:, :plans] + (top[:, plans:] + rest)
    warp(chunks, cores, source_ref, valid_ref, tiles, dose, outs)


def forward(scalars, matrix, tiles, pieces, rows, vox, masks):
    height = tiles.shape[1]
    vox_rows, spots = matrix.shape
    plans = pieces[0].shape[-1]
    cores = core_count()
    out = jax.ShapeDtypeStruct((vox // cores, CAP, height // CHUNKS, plans), F32)
    outs = [out] * (cores * CHUNKS)
    return pl.pallas_call(
        functools.partial(forward_body, (vox, masks, rows, len(pieces), CHUNKS, cores)),
        in_specs=specs(3, pltpu.SMEM) + specs(2 + len(pieces), pltpu.VMEM),
        out_specs=specs(len(outs), pltpu.VMEM),
        out_shape=outs,
        scratch_shapes=[pltpu.VMEM((vox_rows, plans), F32), pltpu.VMEM((spots, 2 * plans), BF16)],
        compiler_params=pltpu.CompilerParams(vmem_limit_bytes=LARGE),
        cost_estimate=BRIEF,
        name="dose_and_warp",
    )(*scalars, matrix, tiles, *pieces)


def piece(arrived, cores, m):
    return arrived[m // cores].at[m % cores]


def gradient_body(dims, source_ref, valid_ref, me_ref, matrix, tiles, *refs):
    vox, masks, rows, cores, chunks = dims
    chips = vox // cores
    returned = refs[: chips * chunks]
    outs = refs[chips * chunks : -3]
    columns, total, turned = refs[-3:]
    height = tiles.shape[1]
    plans = turned.shape[1]
    vox_rows, spots = matrix.shape
    spare = vox_rows // height
    for m in range(vox):
        found = [piece(returned[h * chips : (h + 1) * chips], cores, m) for h in range(chunks)]
        for j in range(CAP):
            s = m * CAP + j
            b = source_ref[s]
            adjoint = jnp.concatenate([f[j] for f in found], axis=0)
            full = jnp.dot(
                halves(adjoint.T, 0), halves(tiles[b], 1), preferred_element_type=F32
            )
            to = jnp.where(valid_ref[s] > 0, b, spare) * height
            columns[:, pl.ds(pl.multiple_of(to, height), height)] = halves(
                term_sum(full, plans, height), 0
            )

    step = min(BLOCK_ROWS_AT_ONCE, vox_rows)
    for first in range(0, vox_rows, step):
        at = slice(first, first + step)
        big, small = terms(matrix[at, :])
        top = jnp.dot(columns[:, at], big, preferred_element_type=F32)
        rest = jnp.dot(columns[:plans, at], small, preferred_element_type=F32)
        part = top[:plans] + (top[plans:] + rest)
        total[...] = part if first == 0 else total[...] + part
    for i in range(0, spots, plans):
        turned[i : i + plans, :] = total[:, i : i + plans].T
    if len(outs[0].shape) == 2:
        outs[0][...] = turned[...]
    else:
        for c in range(cores):
            for k in range(vox // cores):
                for i, p in enumerate(masks):
                    v = me_ref[0] ^ (k * cores + c)
                    at = ((me_ref[1] ^ p) * vox + v) * rows
                    outs[c][k, i * rows : (i + 1) * rows] = turned[
                        pl.ds(pl.multiple_of(at, rows), rows), :
                    ]


def gradient_parts(scalars, matrix, tiles, returned, rows, vox, masks):
    vox_rows, spots = matrix.shape
    plans = returned[0].shape[-1]
    cores = core_count()
    if rows % 8 == 0:
        outs = [jax.ShapeDtypeStruct((vox // cores, len(masks) * rows, plans), F32)] * cores
    else:
        outs = [jax.ShapeDtypeStruct((spots, plans), F32)]
    return pl.pallas_call(
        functools.partial(gradient_body, (vox, masks, rows, cores, CHUNKS)),
        in_specs=specs(3, pltpu.SMEM) + specs(2 + len(returned), pltpu.VMEM),
        out_specs=specs(len(outs), pltpu.VMEM),
        out_shape=outs,
        scratch_shapes=[pltpu.VMEM((2 * plans, vox_rows + tiles.shape[1]), BF16),
            pltpu.VMEM((plans, spots), F32),
            pltpu.VMEM((spots, plans), F32),
        ],
        compiler_params=pltpu.CompilerParams(vmem_limit_bytes=LARGE),
        cost_estimate=BRIEF,
        name="warp_back_and_gradient",
    )(*scalars, matrix, tiles, *returned)


def place_body(vox, cores, which_ref, slot_ref, *refs):
    chips = vox // cores
    arrived, (give, keep, total) = refs[:chips], refs[chips:]
    total[...] = jnp.zeros_like(total)
    for m in range(vox):
        blocks = piece(arrived, cores, m)
        for j in range(CAP):
            slot = slot_ref[m * CAP + j]

            @pl.when(slot >= 0)
            def _():
                total[slot] += blocks[j]

    half = keep.shape[0]
    which = which_ref[0]
    keep[...] = total[pl.ds(which * half, half)]
    give[...] = total[pl.ds((1 - which) * half, half)]


def place(which, slots, incoming, blocks):
    cores = core_count()
    vox = len(incoming) * cores
    height, plans = incoming[0].shape[-2:]
    half = jax.ShapeDtypeStruct((blocks // 2, height, plans), F32)
    return pl.pallas_call(
        functools.partial(place_body, vox, cores),
        in_specs=specs(2, pltpu.SMEM) + specs(len(incoming), pltpu.VMEM),
        out_specs=specs(2, pltpu.VMEM),
        out_shape=[half, half],
        scratch_shapes=[pltpu.VMEM((blocks, height, plans), F32)],
        compiler_params=pltpu.CompilerParams(vmem_limit_bytes=SMALL),
        cost_estimate=BRIEF,
        name="place_blocks",
    )(which, slots, *incoming)


def pull_body(vox, cores, with_dose, ahead, which_ref, slot_ref, mine, other, goal, scale, *refs):
    refs = refs[ahead:]
    half = mine.shape[0]
    which = which_ref[0]
    field = refs[-1]
    field[pl.ds(which * half, half)] = mine[...]
    field[pl.ds((1 - which) * half, half)] = other[...]
    for m in range(vox):
        for j in range(CAP):
            slot = jnp.maximum(slot_ref[m * CAP + j], 0)
            refs[m % cores][m // cores, j] = scale[slot] * (field[slot] - goal[slot])
    if with_dose:
        refs[cores][...] = field[...]


def pull(which, slots, mine, other, goal, scale, vox, with_dose, ahead):
    half, height, plans = mine.shape
    cores = core_count()
    outs = [jax.ShapeDtypeStruct((vox // cores, CAP, height, plans), F32)] * cores
    if with_dose:
        outs = outs + [jax.ShapeDtypeStruct((2 * half, height, plans), F32)]
    return pl.pallas_call(
        functools.partial(pull_body, vox, cores, with_dose, len(ahead)),
        in_specs=specs(2, pltpu.SMEM) + specs(4 + len(ahead), pltpu.VMEM),
        out_specs=specs(len(outs), pltpu.VMEM),
        out_shape=outs,
        scratch_shapes=[pltpu.VMEM((2 * half, height, plans), F32)],
        compiler_params=pltpu.CompilerParams(vmem_limit_bytes=SMALL),
        cost_estimate=BRIEF,
        name="adjoint_blocks",
    )(which, slots, mine, other, goal, scale, *ahead)


def phase_steps():
    count, steps = lax.axis_size(PHASE), []
    while 2 ** len(steps) < count:
        steps.append(2 ** (len(steps) + 1) - 1)
    return steps


def combined(steps):
    masks = [0]
    for s in steps:
        masks += [m ^ s for m in masks]
    return masks


def sum_everywhere(x, axis, steps):
    for i, s in enumerate(steps):
        other = swap(x, axis, s).reshape(-1, 2, 2**i, *x.shape[1:])
        x = x + jnp.concatenate([other[:, 1:], other[:, :1]], axis=1).reshape(x.shape)
    return x


def gather_chips(by_phase):
    cores = core_count()
    by_chip = jnp.stack(spread(by_phase, VOX, range(cores, lax.axis_size(VOX), cores)))
    return spread(by_chip, VOX, range(1, cores))


def sum_chips(parts):
    cores = len(parts)
    chips = parts[0]
    for m in range(1, cores):
        chips = chips + swap(parts[m], VOX, m)
    mine = chips[0]
    for k in range(1, chips.shape[0]):
        mine = mine + swap(chips[k], VOX, k * cores)
    return mine


def cross(pieces):
    cores = len(pieces)
    crossed = [pieces[0]] + [swap(pieces[c], VOX, c) for c in range(1, cores)]
    return [jnp.stack([p[k] for p in crossed]) for k in range(pieces[0].shape[0])]


def send(chips):
    cores = core_count()
    return [chips[0]] + [swap(chips[k], VOX, k * cores) for k in range(1, len(chips))]


def exchange(pieces):
    return send(cross(pieces))


def hold_body(matrix, x, out):
    out[...] = x[0, :8, :]


def hold(matrix, x):
    return pl.pallas_call(
        hold_body,
        in_specs=specs(2, pltpu.VMEM),
        out_specs=pl.BlockSpec(memory_space=pltpu.VMEM),
        out_shape=jax.ShapeDtypeStruct((8, x.shape[-1]), F32),
        compiler_params=pltpu.CompilerParams(vmem_limit_bytes=SMALL),
        cost_estimate=BRIEF,
        name="hold",
    )(matrix, x)


def phase_stages(half):
    for step in phase_steps()[1:-1]:
        half = half + swap(half, PHASE, step)
    return half, swap(half, PHASE, phase_steps()[-1])


def tie(x, other):
    return lax.optimization_barrier((x, other))[0]


def goals_and_scales(structure, prescribed, importance, blocks, height):
    highest = lax.Precision.HIGHEST
    member = (structure[:, None] == jnp.arange(NSTRUCT, dtype=jnp.int32)[None, :]).astype(F32)
    target_dose = jnp.dot(member, prescribed, precision=highest, preferred_element_type=F32)
    voxel_weight = jnp.dot(
        member, importance[:, None], precision=highest, preferred_element_type=F32
    )
    voxel_weight = jnp.broadcast_to(voxel_weight, target_dose.shape)
    shape = (blocks, CHUNKS, height // CHUNKS, prescribed.shape[1])
    cut = [x.reshape(shape) for x in (target_dose, voxel_weight)]
    return [[x[:, h] for h in range(CHUNKS)] for x in cut]


def per_device(
    influence,
    weights,
    warp_tiles,
    owners,
    owner_slot,
    tile_index,
    structure,
    prescribed,
    importance,
    step_size,
):
    matrix = influence[0]
    vox_rows, spots = matrix.shape
    block_rows = warp_tiles.shape[1]
    rows, plans = weights.shape
    local_blocks = vox_rows // block_rows
    vox = lax.axis_size(VOX)
    phases = lax.axis_size(PHASE)
    cores = core_count()
    me_vox = lax.axis_index(VOX)
    me_phase = lax.axis_index(PHASE)
    slots_all = vox * CAP
    targets = owners[0, :, 0]
    which = ((me_phase ^ (me_phase >> 1)) & 1).astype(jnp.int32).reshape(1)

    def orders(names):
        before = jnp.tril(jnp.ones((local_blocks, local_blocks), jnp.int32), -1)
        same = (names[..., :, None] == names[..., None, :]).astype(jnp.int32)
        return jnp.sum(same * before, axis=-1)

    position = (targets ^ me_vox) * CAP + orders(targets)
    chosen_mask = jnp.arange(slots_all, dtype=jnp.int32)[:, None] == position[None, :]
    positions_i = jnp.arange(local_blocks, dtype=jnp.int32)
    source = jnp.sum(jnp.where(chosen_mask, positions_i[None, :], 0), axis=1)
    valid = jnp.sum(chosen_mask.astype(jnp.int32), axis=1)
    me = jnp.stack([me_vox, me_phase]).astype(jnp.int32)
    scalars = (source, valid, me)
    labels = jnp.zeros((LABEL_ROWS, plans), F32)
    labels = labels.at[0, :local_blocks].set(targets.astype(F32))
    labels = labels.at[1, :local_blocks].set(owner_slot[0].astype(F32))

    masks = combined(phase_steps())
    tiles = warp_tiles[tile_index[0]]
    held = jnp.concatenate(spread(weights, PHASE, masks[1:]), axis=0)
    for iteration in range(ITERS):
        last = iteration == ITERS - 1
        if iteration == 0:
            pieces = gather_chips(jnp.concatenate([held, labels], axis=0))
            infos = jnp.stack(pieces, axis=1).reshape(vox, -1, plans)[:, phases * rows :]
            names = infos[:, 0, :local_blocks].astype(jnp.int32)
            slots = infos[:, 1, :local_blocks].astype(jnp.int32)
            order = jnp.where(names == me_vox, orders(names), -1)
            hit = order[:, None, :] == jnp.arange(CAP, dtype=jnp.int32)[None, :, None]
            received = jnp.sum(jnp.where(hit, slots[:, None, :] + 1, 0), axis=-1)
            received = received.reshape(slots_all) - 1
        else:
            pieces = gather_chips(held)
        if rows % 16:
            every = jnp.stack(pieces, axis=1).reshape(vox, -1, plans)[:, : phases * rows]
            every = every.reshape(vox, phases, rows, plans)
            back_to = jnp.asarray([masks.index(p) for p in range(phases)], jnp.int32)
            every = every[jnp.arange(vox) ^ me_vox][:, back_to[jnp.arange(phases) ^ me_phase]]
            pieces = [every.transpose(1, 0, 2, 3).reshape(spots, plans)]
        outgoing = forward(scalars, matrix, tiles, pieces, rows, vox, masks)
        returned, dose = [], []
        incoming, held_halves, seconds = exchange(outgoing[:cores]), [], []
        for h in range(CHUNKS):
            give, keep = place(which, received, incoming, local_blocks)
            got = swap(give, PHASE, 1)
            if iteration == 0 and h == 0:
                goals, scales = goals_and_scales(
                    tie(structure, give), prescribed, importance, local_blocks, block_rows
                )
            if h + 1 < CHUNKS:
                later = outgoing[(h + 1) * cores : (h + 2) * cores]
                incoming = exchange([tie(x, incoming[2]) for x in later])
            if h > 0:
                got = tie(got, seconds[-1])
            half, second = phase_stages(keep + got)
            held_halves.append(half)
            seconds.append(second)
        for h in range(CHUNKS):
            second = seconds[h] if h == 0 else tie(seconds[h], other)
            mine = held_halves[h] + second
            other = swap(mine, PHASE, 1)
            ahead = [hold(matrix, held_halves[1])] if iteration == 0 and h == 0 else []
            back = pull(which, received, mine, other, goals[h], scales[h], vox, last, ahead)
            returned += exchange(back[:cores])
            dose += back[cores:]
        parts = gradient_parts(scalars, matrix, tiles, returned, rows, vox, masks)
        if rows % 8:
            parts = parts[0].reshape(phases, vox, rows, plans)
            wanted = jnp.asarray(masks, jnp.int32) ^ me_phase
            parts = parts[wanted][:, jnp.arange(vox) ^ me_vox]
            parts = parts.transpose(1, 0, 2, 3).reshape(vox // cores, cores, phases * rows, plans)
            parts = [parts[:, c] for c in range(cores)]
        total = sum_chips(parts)
        if last:
            split = total.reshape(phases, rows, plans)
            total = split[0]
            for i, m in enumerate(masks[1:], 1):
                total = total + swap(split[i], PHASE, m)
            new_weights = jnp.maximum(held[:rows] - step_size[None, :] * total, 0.0)
        else:
            total = sum_everywhere(total.reshape(phases, rows, plans), PHASE, phase_steps())
            held = jnp.maximum(held - step_size[None, :] * total.reshape(held.shape), 0.0)
    dose_field = jnp.stack(dose, axis=1).reshape(vox_rows, plans)
    return (new_weights, dose_field)


def solution(mesh):
    in_specs = (
        P("phase", "vox", None),
        P(("phase", "vox"), None),
        P(),
        P("phase", "vox", None),
        P("phase", "vox"),
        P("phase", "vox"),
        P("vox"),
        P(),
        P(),
        P(),
    )
    out_specs = (P(("phase", "vox"), None), P("vox", None))
    return jax.shard_map(
        per_device, mesh=mesh, in_specs=in_specs, out_specs=out_specs, check_vma=False
    )
```

```python
import functools

import jax
import jax.numpy as jnp
from jax import lax
from jax.experimental import pallas as pl
from jax.experimental.pallas import tpu as pltpu
from jax.sharding import PartitionSpec as P

CAP = 2
NSTRUCT = 8
ITERS = 2
CHUNKS = 2
VOX = "vox"
PHASE = "phase"
LABEL_ROWS = 16
F32 = jnp.float32
BF16 = jnp.bfloat16
LARGE = 14 << 20
SMALL = 4 << 20
ROWS_AT_ONCE = 512
BLOCK_ROWS_AT_ONCE = 256
BRIEF = pl.CostEstimate(flops=1, bytes_accessed=1, transcendentals=0)


def swap(x, axis, mask):
    count = lax.axis_size(axis)
    return lax.ppermute(x, axis, [(i, i ^ mask) for i in range(count)])


def spread(x, axis, masks):
    return [x] + [swap(x, axis, m) for m in masks]


def core_count():
    return min(2, lax.axis_size(VOX))


def terms(x):
    big = x.astype(BF16)
    return big, (x - big.astype(F32)).astype(BF16)


def halves(x, axis):
    return jnp.concatenate(terms(x), axis=axis)


def term_sum(full, rows, cols):
    return full[:rows, :cols] + (full[:rows, cols:] + full[rows:, :cols])


def specs(count, space):
    return [pl.BlockSpec(memory_space=space)] * count


def fill_weights(me_ref, out, pieces, rows, vox, masks):
    cores = len(pieces)
    for c, ref in enumerate(pieces):
        for k in range(vox // cores):
            for i, p in enumerate(masks):
                v = me_ref[0] ^ (k * cores + c)
                at = ((me_ref[1] ^ p) * vox + v) * rows
                out[pl.ds(pl.multiple_of(at, rows), rows), :] = halves(
                    ref[k, i * rows : (i + 1) * rows, :], 1
                )


def warp(chunks, cores, source_ref, valid_ref, tiles, dose, outs):
    height = tiles.shape[1]
    plans = dose.shape[1]
    part = height // chunks
    for c in range(cores):
        for k in range(outs[0].shape[0]):
            for j in range(CAP):
                s = (k * cores + c) * CAP + j
                b = source_ref[s]
                block = dose[pl.ds(pl.multiple_of(b * height, height), height), :]
                full = jnp.dot(
                    halves(tiles[b], 0), halves(block, 1), preferred_element_type=F32
                )
                warped = jnp.where(valid_ref[s] > 0, term_sum(full, height, plans), 0.0)
                for h in range(chunks):
                    outs[h * cores + c][k, j] = warped[h * part : (h + 1) * part]


def forward_body(dims, ahead, source_ref, valid_ref, me_ref, matrix, tiles, *refs):
    refs = refs[ahead:]
    vox, masks, rows, pieces_n, chunks, cores = dims
    pieces, outs = refs[:pieces_n], refs[pieces_n:-2]
    dose, weights = refs[-2:]
    plans = dose.shape[1]
    if len(pieces[0].shape) == 2:
        weights[...] = halves(pieces[0][...], 1)
    else:
        fill_weights(me_ref, weights, pieces, rows, vox, masks)
    step = min(ROWS_AT_ONCE, dose.shape[0])
    for first in range(0, dose.shape[0], step):
        at = slice(first, first + step)
        big, small = terms(matrix[at, :])
        top = jnp.dot(big, weights[...], preferred_element_type=F32)
        rest = jnp.dot(small, weights[:, :plans], preferred_element_type=F32)
        dose[at, :] = top[:, :plans] + (top[:, plans:] + rest)
    warp(chunks, cores, source_ref, valid_ref, tiles, dose, outs)


def forward(scalars, matrix, tiles, pieces, rows, vox, masks, ahead):
    height = tiles.shape[1]
    vox_rows, spots = matrix.shape
    plans = pieces[0].shape[-1]
    cores = core_count()
    out = jax.ShapeDtypeStruct((vox // cores, CAP, height // CHUNKS, plans), F32)
    outs = [out] * (cores * CHUNKS)
    return pl.pallas_call(
        functools.partial(
            forward_body, (vox, masks, rows, len(pieces), CHUNKS, cores), len(ahead)
        ),
        in_specs=specs(3, pltpu.SMEM) + specs(2 + len(ahead) + len(pieces), pltpu.VMEM),
        out_specs=specs(len(outs), pltpu.VMEM),
        out_shape=outs,
        scratch_shapes=[pltpu.VMEM((vox_rows, plans), F32), pltpu.VMEM((spots, 2 * plans), BF16)],
        compiler_params=pltpu.CompilerParams(vmem_limit_bytes=LARGE),
        cost_estimate=BRIEF,
        name="dose_and_warp",
    )(*scalars, matrix, tiles, *ahead, *pieces)


def piece(arrived, cores, m):
    return arrived[m // cores].at[m % cores]


def gradient_body(dims, source_ref, valid_ref, me_ref, matrix, tiles, *refs):
    vox, masks, rows, cores, chunks = dims
    chips = vox // cores
    returned = refs[: chips * chunks]
    outs = refs[chips * chunks : -3]
    columns, total, turned = refs[-3:]
    height = tiles.shape[1]
    plans = turned.shape[1]
    vox_rows, spots = matrix.shape
    spare = vox_rows // height
    for m in range(vox):
        found = [piece(returned[h * chips : (h + 1) * chips], cores, m) for h in range(chunks)]
        for j in range(CAP):
            s = m * CAP + j
            b = source_ref[s]
            adjoint = jnp.concatenate([f[j] for f in found], axis=0)
            full = jnp.dot(
                halves(adjoint.T, 0), halves(tiles[b], 1), preferred_element_type=F32
            )
            to = jnp.where(valid_ref[s] > 0, b, spare) * height
            columns[:, pl.ds(pl.multiple_of(to, height), height)] = halves(
                term_sum(full, plans, height), 0
            )

    step = min(BLOCK_ROWS_AT_ONCE, vox_rows)
    for first in range(0, vox_rows, step):
        at = slice(first, first + step)
        big, small = terms(matrix[at, :])
        top = jnp.dot(columns[:, at], big, preferred_element_type=F32)
        rest = jnp.dot(columns[:plans, at], small, preferred_element_type=F32)
        part = top[:plans] + (top[plans:] + rest)
        total[...] = part if first == 0 else total[...] + part
    for i in range(0, spots, plans):
        turned[i : i + plans, :] = total[:, i : i + plans].T
    if len(outs[0].shape) == 2:
        outs[0][...] = turned[...]
    else:
        for c in range(cores):
            for k in range(vox // cores):
                for i, p in enumerate(masks):
                    v = me_ref[0] ^ (k * cores + c)
                    at = ((me_ref[1] ^ p) * vox + v) * rows
                    outs[c][k, i * rows : (i + 1) * rows] = turned[
                        pl.ds(pl.multiple_of(at, rows), rows), :
                    ]


def gradient_parts(scalars, matrix, tiles, returned, rows, vox, masks):
    vox_rows, spots = matrix.shape
    plans = returned[0].shape[-1]
    cores = core_count()
    if rows % 8 == 0:
        outs = [jax.ShapeDtypeStruct((vox // cores, len(masks) * rows, plans), F32)] * cores
    else:
        outs = [jax.ShapeDtypeStruct((spots, plans), F32)]
    return pl.pallas_call(
        functools.partial(gradient_body, (vox, masks, rows, cores, CHUNKS)),
        in_specs=specs(3, pltpu.SMEM) + specs(2 + len(returned), pltpu.VMEM),
        out_specs=specs(len(outs), pltpu.VMEM),
        out_shape=outs,
        scratch_shapes=[pltpu.VMEM((2 * plans, vox_rows + tiles.shape[1]), BF16),
            pltpu.VMEM((plans, spots), F32),
            pltpu.VMEM((spots, plans), F32),
        ],
        compiler_params=pltpu.CompilerParams(vmem_limit_bytes=LARGE),
        cost_estimate=BRIEF,
        name="warp_back_and_gradient",
    )(*scalars, matrix, tiles, *returned)


def place_body(vox, cores, which_ref, slot_ref, *refs):
    chips = vox // cores
    arrived, (give, keep, total) = refs[:chips], refs[chips:]
    total[...] = jnp.zeros_like(total)
    for m in range(vox):
        blocks = piece(arrived, cores, m)
        for j in range(CAP):
            slot = slot_ref[m * CAP + j]

            @pl.when(slot >= 0)
            def _():
                total[slot] += blocks[j]

    half = keep.shape[0]
    which = which_ref[0]
    keep[...] = total[pl.ds(which * half, half)]
    give[...] = total[pl.ds((1 - which) * half, half)]


def place(which, slots, incoming, blocks):
    cores = core_count()
    vox = len(incoming) * cores
    height, plans = incoming[0].shape[-2:]
    half = jax.ShapeDtypeStruct((blocks // 2, height, plans), F32)
    return pl.pallas_call(
        functools.partial(place_body, vox, cores),
        in_specs=specs(2, pltpu.SMEM) + specs(len(incoming), pltpu.VMEM),
        out_specs=specs(2, pltpu.VMEM),
        out_shape=[half, half],
        scratch_shapes=[pltpu.VMEM((blocks, height, plans), F32)],
        compiler_params=pltpu.CompilerParams(vmem_limit_bytes=SMALL),
        cost_estimate=BRIEF,
        name="place_blocks",
    )(which, slots, *incoming)


def pull_body(vox, cores, with_dose, ahead, which_ref, slot_ref, mine, other, goal, scale, *refs):
    refs = refs[ahead:]
    half = mine.shape[0]
    which = which_ref[0]
    field = refs[-1]
    field[pl.ds(which * half, half)] = mine[...]
    field[pl.ds((1 - which) * half, half)] = other[...]
    for m in range(vox):
        for j in range(CAP):
            slot = jnp.maximum(slot_ref[m * CAP + j], 0)
            refs[m % cores][m // cores, j] = scale[slot] * (field[slot] - goal[slot])
    if with_dose:
        refs[cores][...] = field[...]


def pull(which, slots, mine, other, goal, scale, vox, with_dose, ahead):
    half, height, plans = mine.shape
    cores = core_count()
    outs = [jax.ShapeDtypeStruct((vox // cores, CAP, height, plans), F32)] * cores
    if with_dose:
        outs = outs + [jax.ShapeDtypeStruct((2 * half, height, plans), F32)]
    return pl.pallas_call(
        functools.partial(pull_body, vox, cores, with_dose, len(ahead)),
        in_specs=specs(2, pltpu.SMEM) + specs(4 + len(ahead), pltpu.VMEM),
        out_specs=specs(len(outs), pltpu.VMEM),
        out_shape=outs,
        scratch_shapes=[pltpu.VMEM((2 * half, height, plans), F32)],
        compiler_params=pltpu.CompilerParams(vmem_limit_bytes=SMALL),
        cost_estimate=BRIEF,
        name="adjoint_blocks",
    )(which, slots, mine, other, goal, scale, *ahead)


def phase_steps():
    count, steps = lax.axis_size(PHASE), []
    while 2 ** len(steps) < count:
        steps.append(2 ** (len(steps) + 1) - 1)
    return steps


def combined(steps):
    masks = [0]
    for s in steps:
        masks += [m ^ s for m in masks]
    return masks


def sum_everywhere(x, axis, steps):
    for i, s in enumerate(steps):
        other = swap(x, axis, s).reshape(-1, 2, 2**i, *x.shape[1:])
        x = x + jnp.concatenate([other[:, 1:], other[:, :1]], axis=1).reshape(x.shape)
    return x


def gather_chips(by_phase):
    cores = core_count()
    by_chip = jnp.stack(spread(by_phase, VOX, range(cores, lax.axis_size(VOX), cores)))
    return spread(by_chip, VOX, range(1, cores))


def sum_chips(parts):
    cores = len(parts)
    chips = parts[0]
    for m in range(1, cores):
        chips = chips + swap(parts[m], VOX, m)
    mine = chips[0]
    for k in range(1, chips.shape[0]):
        mine = mine + swap(chips[k], VOX, k * cores)
    return mine


def cross(pieces):
    cores = len(pieces)
    crossed = [pieces[0]] + [swap(pieces[c], VOX, c) for c in range(1, cores)]
    return [jnp.stack([p[k] for p in crossed]) for k in range(pieces[0].shape[0])]


def send(chips):
    cores = core_count()
    return [chips[0]] + [swap(chips[k], VOX, k * cores) for k in range(1, len(chips))]


def exchange(pieces):
    return send(cross(pieces))


def hold_body(matrix, x, out):
    out[...] = x[0, :8, :]


def hold(matrix, x):
    return pl.pallas_call(
        hold_body,
        in_specs=specs(2, pltpu.VMEM),
        out_specs=pl.BlockSpec(memory_space=pltpu.VMEM),
        out_shape=jax.ShapeDtypeStruct((8, x.shape[-1]), F32),
        compiler_params=pltpu.CompilerParams(vmem_limit_bytes=LARGE),
        cost_estimate=BRIEF,
        name="hold",
    )(matrix, x)


def phase_stages(half):
    for step in phase_steps()[1:-1]:
        half = half + swap(half, PHASE, step)
    return half, swap(half, PHASE, phase_steps()[-1])


def tie(x, other):
    return lax.optimization_barrier((x, other))[0]


def goals_and_scales(structure, prescribed, importance, blocks, height):
    highest = lax.Precision.HIGHEST
    member = (structure[:, None] == jnp.arange(NSTRUCT, dtype=jnp.int32)[None, :]).astype(F32)
    target_dose = jnp.dot(member, prescribed, precision=highest, preferred_element_type=F32)
    voxel_weight = jnp.dot(
        member, importance[:, None], precision=highest, preferred_element_type=F32
    )
    voxel_weight = jnp.broadcast_to(voxel_weight, target_dose.shape)
    shape = (blocks, CHUNKS, height // CHUNKS, prescribed.shape[1])
    cut = [x.reshape(shape) for x in (target_dose, voxel_weight)]
    return [[x[:, h] for h in range(CHUNKS)] for x in cut]


def per_device(
    influence,
    weights,
    warp_tiles,
    owners,
    owner_slot,
    tile_index,
    structure,
    prescribed,
    importance,
    step_size,
):
    matrix = influence[0]
    vox_rows, spots = matrix.shape
    block_rows = warp_tiles.shape[1]
    rows, plans = weights.shape
    local_blocks = vox_rows // block_rows
    vox = lax.axis_size(VOX)
    phases = lax.axis_size(PHASE)
    cores = core_count()
    me_vox = lax.axis_index(VOX)
    me_phase = lax.axis_index(PHASE)
    slots_all = vox * CAP
    targets = owners[0, :, 0]
    which = ((me_phase ^ (me_phase >> 1)) & 1).astype(jnp.int32).reshape(1)

    def orders(names):
        before = jnp.tril(jnp.ones((local_blocks, local_blocks), jnp.int32), -1)
        same = (names[..., :, None] == names[..., None, :]).astype(jnp.int32)
        return jnp.sum(same * before, axis=-1)

    position = (targets ^ me_vox) * CAP + orders(targets)
    chosen_mask = jnp.arange(slots_all, dtype=jnp.int32)[:, None] == position[None, :]
    positions_i = jnp.arange(local_blocks, dtype=jnp.int32)
    source = jnp.sum(jnp.where(chosen_mask, positions_i[None, :], 0), axis=1)
    valid = jnp.sum(chosen_mask.astype(jnp.int32), axis=1)
    me = jnp.stack([me_vox, me_phase]).astype(jnp.int32)
    scalars = (source, valid, me)
    labels = jnp.zeros((LABEL_ROWS, plans), F32)
    labels = labels.at[0, :local_blocks].set(targets.astype(F32))
    labels = labels.at[1, :local_blocks].set(owner_slot[0].astype(F32))

    masks = combined(phase_steps())
    tiles = warp_tiles[tile_index[0]]
    held = jnp.concatenate(spread(weights, PHASE, masks[1:]), axis=0)
    for iteration in range(ITERS):
        last = iteration == ITERS - 1
        if iteration == 0:
            pieces = gather_chips(jnp.concatenate([held, labels], axis=0))
            infos = jnp.stack(pieces, axis=1).reshape(vox, -1, plans)[:, phases * rows :]
            names = infos[:, 0, :local_blocks].astype(jnp.int32)
            slots = infos[:, 1, :local_blocks].astype(jnp.int32)
            order = jnp.where(names == me_vox, orders(names), -1)
            hit = order[:, None, :] == jnp.arange(CAP, dtype=jnp.int32)[None, :, None]
            received = jnp.sum(jnp.where(hit, slots[:, None, :] + 1, 0), axis=-1)
            received = received.reshape(slots_all) - 1
        else:
            pieces = gather_chips(held)
        if rows % 16:
            every = jnp.stack(pieces, axis=1).reshape(vox, -1, plans)[:, : phases * rows]
            every = every.reshape(vox, phases, rows, plans)
            back_to = jnp.asarray([masks.index(p) for p in range(phases)], jnp.int32)
            every = every[jnp.arange(vox) ^ me_vox][:, back_to[jnp.arange(phases) ^ me_phase]]
            pieces = [every.transpose(1, 0, 2, 3).reshape(spots, plans)]
        ahead = [hold(matrix, held[None])] if iteration == 0 else []
        outgoing = forward(scalars, matrix, tiles, pieces, rows, vox, masks, ahead)
        returned, dose = [], []
        incoming, held_halves, seconds = exchange(outgoing[:cores]), [], []
        for h in range(CHUNKS):
            give, keep = place(which, received, incoming, local_blocks)
            got = swap(give, PHASE, 1)
            if iteration == 0 and h == 0:
                goals, scales = goals_and_scales(
                    tie(structure, give), prescribed, importance, local_blocks, block_rows
                )
            if h + 1 < CHUNKS:
                later = outgoing[(h + 1) * cores : (h + 2) * cores]
                incoming = exchange([tie(x, incoming[2]) for x in later])
            if h > 0:
                got = tie(got, seconds[-1])
            half, second = phase_stages(keep + got)
            held_halves.append(half)
            seconds.append(second)
        for h in range(CHUNKS):
            second = seconds[h] if h == 0 else tie(seconds[h], other)
            mine = held_halves[h] + second
            other = swap(mine, PHASE, 1)
            ahead = [hold(matrix, held_halves[1])] if iteration == 0 and h == 0 else []
            back = pull(which, received, mine, other, goals[h], scales[h], vox, last, ahead)
            returned += exchange(back[:cores])
            dose += back[cores:]
        parts = gradient_parts(scalars, matrix, tiles, returned, rows, vox, masks)
        if rows % 8:
            parts = parts[0].reshape(phases, vox, rows, plans)
            wanted = jnp.asarray(masks, jnp.int32) ^ me_phase
            parts = parts[wanted][:, jnp.arange(vox) ^ me_vox]
            parts = parts.transpose(1, 0, 2, 3).reshape(vox // cores, cores, phases * rows, plans)
            parts = [parts[:, c] for c in range(cores)]
        total = sum_chips(parts)
        if last:
            split = total.reshape(phases, rows, plans)
            total = split[0]
            for i, m in enumerate(masks[1:], 1):
                total = total + swap(split[i], PHASE, m)
            new_weights = jnp.maximum(held[:rows] - step_size[None, :] * total, 0.0)
        else:
            total = sum_everywhere(total.reshape(phases, rows, plans), PHASE, phase_steps())
            held = jnp.maximum(held - step_size[None, :] * total.reshape(held.shape), 0.0)
    dose_field = jnp.stack(dose, axis=1).reshape(vox_rows, plans)
    return (new_weights, dose_field)


def solution(mesh):
    in_specs = (
        P("phase", "vox", None),
        P(("phase", "vox"), None),
        P(),
        P("phase", "vox", None),
        P("phase", "vox"),
        P("phase", "vox"),
        P("vox"),
        P(),
        P(),
        P(),
    )
    out_specs = (P(("phase", "vox"), None), P("vox", None))
    return jax.shard_map(
        per_device, mesh=mesh, in_specs=in_specs, out_specs=out_specs, check_vma=False
    )
```

```python
import functools

import jax
import jax.numpy as jnp
from jax import lax
from jax.experimental import pallas as pl
from jax.experimental.pallas import tpu as pltpu
from jax.sharding import PartitionSpec as P

CAP = 2
NSTRUCT = 8
ITERS = 2
CHUNKS = 2
VOX = "vox"
PHASE = "phase"
LABEL_ROWS = 16
F32 = jnp.float32
BF16 = jnp.bfloat16
LARGE = 14 << 20
SMALL = 4 << 20
ROWS_AT_ONCE = 512
BLOCK_ROWS_AT_ONCE = 256
BRIEF = pl.CostEstimate(flops=1, bytes_accessed=1, transcendentals=0)


def swap(x, axis, mask):
    count = lax.axis_size(axis)
    return lax.ppermute(x, axis, [(i, i ^ mask) for i in range(count)])


def spread(x, axis, masks):
    return [x] + [swap(x, axis, m) for m in masks]


def core_count():
    return min(2, lax.axis_size(VOX))


def terms(x):
    big = x.astype(BF16)
    return big, (x - big.astype(F32)).astype(BF16)


def halves(x, axis):
    return jnp.concatenate(terms(x), axis=axis)


def term_sum(full, rows, cols):
    return full[:rows, :cols] + (full[:rows, cols:] + full[rows:, :cols])


def specs(count, space):
    return [pl.BlockSpec(memory_space=space)] * count


def fill_weights(me_ref, out, pieces, rows, vox, masks):
    cores = len(pieces)
    for c, ref in enumerate(pieces):
        for k in range(vox // cores):
            for i, p in enumerate(masks):
                v = me_ref[0] ^ (k * cores + c)
                at = ((me_ref[1] ^ p) * vox + v) * rows
                out[pl.ds(pl.multiple_of(at, rows), rows), :] = halves(
                    ref[k, i * rows : (i + 1) * rows, :], 1
                )


def warp(chunks, cores, source_ref, valid_ref, tiles, dose, outs):
    height = tiles.shape[1]
    plans = dose.shape[1]
    part = height // chunks
    for c in range(cores):
        for k in range(outs[0].shape[0]):
            for j in range(CAP):
                s = (k * cores + c) * CAP + j
                b = source_ref[s]
                block = dose[pl.ds(pl.multiple_of(b * height, height), height), :]
                full = jnp.dot(
                    halves(tiles[b], 0), halves(block, 1), preferred_element_type=F32
                )
                warped = jnp.where(valid_ref[s] > 0, term_sum(full, height, plans), 0.0)
                for h in range(chunks):
                    outs[h * cores + c][k, j] = warped[h * part : (h + 1) * part]


def forward_body(dims, ahead, source_ref, valid_ref, me_ref, matrix, tiles, *refs):
    refs = refs[ahead:]
    vox, masks, rows, pieces_n, chunks, cores = dims
    pieces, outs = refs[:pieces_n], refs[pieces_n:-2]
    dose, weights = refs[-2:]
    plans = dose.shape[1]
    if len(pieces[0].shape) == 2:
        weights[...] = halves(pieces[0][...], 1)
    else:
        fill_weights(me_ref, weights, pieces, rows, vox, masks)
    step = min(ROWS_AT_ONCE, dose.shape[0])
    for first in range(0, dose.shape[0], step):
        at = slice(first, first + step)
        big, small = terms(matrix[at, :])
        top = jnp.dot(big, weights[...], preferred_element_type=F32)
        rest = jnp.dot(small, weights[:, :plans], preferred_element_type=F32)
        dose[at, :] = top[:, :plans] + (top[:, plans:] + rest)
    warp(chunks, cores, source_ref, valid_ref, tiles, dose, outs)


def forward(scalars, matrix, tiles, pieces, rows, vox, masks, ahead):
    height = tiles.shape[1]
    vox_rows, spots = matrix.shape
    plans = pieces[0].shape[-1]
    cores = core_count()
    out = jax.ShapeDtypeStruct((vox // cores, CAP, height // CHUNKS, plans), F32)
    outs = [out] * (cores * CHUNKS)
    return pl.pallas_call(
        functools.partial(
            forward_body, (vox, masks, rows, len(pieces), CHUNKS, cores), len(ahead)
        ),
        in_specs=specs(3, pltpu.SMEM) + specs(2 + len(ahead) + len(pieces), pltpu.VMEM),
        out_specs=specs(len(outs), pltpu.VMEM),
        out_shape=outs,
        scratch_shapes=[pltpu.VMEM((vox_rows, plans), F32), pltpu.VMEM((spots, 2 * plans), BF16)],
        compiler_params=pltpu.CompilerParams(vmem_limit_bytes=LARGE),
        cost_estimate=BRIEF,
        name="dose_and_warp",
    )(*scalars, matrix, tiles, *ahead, *pieces)


def piece(arrived, cores, m):
    return arrived[m // cores].at[m % cores]


def gradient_body(dims, source_ref, valid_ref, me_ref, matrix, tiles, *refs):
    vox, masks, rows, cores, chunks = dims
    chips = vox // cores
    returned = refs[: chips * chunks]
    outs = refs[chips * chunks : -3]
    columns, total, turned = refs[-3:]
    height = tiles.shape[1]
    plans = turned.shape[1]
    vox_rows, spots = matrix.shape
    spare = vox_rows // height
    for m in range(vox):
        found = [piece(returned[h * chips : (h + 1) * chips], cores, m) for h in range(chunks)]
        for j in range(CAP):
            s = m * CAP + j
            b = source_ref[s]
            adjoint = jnp.concatenate([f[j] for f in found], axis=0)
            full = jnp.dot(
                halves(adjoint.T, 0), halves(tiles[b], 1), preferred_element_type=F32
            )
            to = jnp.where(valid_ref[s] > 0, b, spare) * height
            columns[:, pl.ds(pl.multiple_of(to, height), height)] = halves(
                term_sum(full, plans, height), 0
            )

    step = min(BLOCK_ROWS_AT_ONCE, vox_rows)
    for first in range(0, vox_rows, step):
        at = slice(first, first + step)
        big, small = terms(matrix[at, :])
        top = jnp.dot(columns[:, at], big, preferred_element_type=F32)
        rest = jnp.dot(columns[:plans, at], small, preferred_element_type=F32)
        part = top[:plans] + (top[plans:] + rest)
        total[...] = part if first == 0 else total[...] + part
    for i in range(0, spots, plans):
        turned[i : i + plans, :] = total[:, i : i + plans].T
    if len(outs[0].shape) == 2:
        outs[0][...] = turned[...]
    else:
        for c in range(cores):
            for k in range(vox // cores):
                for i, p in enumerate(masks):
                    v = me_ref[0] ^ (k * cores + c)
                    at = ((me_ref[1] ^ p) * vox + v) * rows
                    outs[c][k, i * rows : (i + 1) * rows] = turned[
                        pl.ds(pl.multiple_of(at, rows), rows), :
                    ]


def gradient_parts(scalars, matrix, tiles, returned, rows, vox, masks):
    vox_rows, spots = matrix.shape
    plans = returned[0].shape[-1]
    cores = core_count()
    if rows % 8 == 0:
        outs = [jax.ShapeDtypeStruct((vox // cores, len(masks) * rows, plans), F32)] * cores
    else:
        outs = [jax.ShapeDtypeStruct((spots, plans), F32)]
    return pl.pallas_call(
        functools.partial(gradient_body, (vox, masks, rows, cores, CHUNKS)),
        in_specs=specs(3, pltpu.SMEM) + specs(2 + len(returned), pltpu.VMEM),
        out_specs=specs(len(outs), pltpu.VMEM),
        out_shape=outs,
        scratch_shapes=[pltpu.VMEM((2 * plans, vox_rows + tiles.shape[1]), BF16),
            pltpu.VMEM((plans, spots), F32),
            pltpu.VMEM((spots, plans), F32),
        ],
        compiler_params=pltpu.CompilerParams(vmem_limit_bytes=LARGE),
        cost_estimate=BRIEF,
        name="warp_back_and_gradient",
    )(*scalars, matrix, tiles, *returned)


def place_body(vox, cores, which_ref, slot_ref, *refs):
    chips = vox // cores
    arrived, (give, keep, total) = refs[:chips], refs[chips:]
    total[...] = jnp.zeros_like(total)
    for m in range(vox):
        blocks = piece(arrived, cores, m)
        for j in range(CAP):
            slot = slot_ref[m * CAP + j]

            @pl.when(slot >= 0)
            def _():
                total[slot] += blocks[j]

    half = keep.shape[0]
    which = which_ref[0]
    keep[...] = total[pl.ds(which * half, half)]
    give[...] = total[pl.ds((1 - which) * half, half)]


def place(which, slots, incoming, blocks):
    cores = core_count()
    vox = len(incoming) * cores
    height, plans = incoming[0].shape[-2:]
    half = jax.ShapeDtypeStruct((blocks // 2, height, plans), F32)
    return pl.pallas_call(
        functools.partial(place_body, vox, cores),
        in_specs=specs(2, pltpu.SMEM) + specs(len(incoming), pltpu.VMEM),
        out_specs=specs(2, pltpu.VMEM),
        out_shape=[half, half],
        scratch_shapes=[pltpu.VMEM((blocks, height, plans), F32)],
        compiler_params=pltpu.CompilerParams(vmem_limit_bytes=SMALL),
        cost_estimate=BRIEF,
        name="place_blocks",
    )(which, slots, *incoming)


def pull_body(vox, cores, with_dose, ahead, which_ref, slot_ref, mine, other, goal, scale, *refs):
    refs = refs[ahead:]
    half = mine.shape[0]
    which = which_ref[0]
    field = refs[-1]
    field[pl.ds(which * half, half)] = mine[...]
    field[pl.ds((1 - which) * half, half)] = other[...]
    for m in range(vox):
        for j in range(CAP):
            slot = jnp.maximum(slot_ref[m * CAP + j], 0)
            refs[m % cores][m // cores, j] = scale[slot] * (field[slot] - goal[slot])
    if with_dose:
        refs[cores][...] = field[...]


def pull(which, slots, mine, other, goal, scale, vox, with_dose, ahead):
    half, height, plans = mine.shape
    cores = core_count()
    outs = [jax.ShapeDtypeStruct((vox // cores, CAP, height, plans), F32)] * cores
    if with_dose:
        outs = outs + [jax.ShapeDtypeStruct((2 * half, height, plans), F32)]
    return pl.pallas_call(
        functools.partial(pull_body, vox, cores, with_dose, len(ahead)),
        in_specs=specs(2, pltpu.SMEM) + specs(4 + len(ahead), pltpu.VMEM),
        out_specs=specs(len(outs), pltpu.VMEM),
        out_shape=outs,
        scratch_shapes=[pltpu.VMEM((2 * half, height, plans), F32)],
        compiler_params=pltpu.CompilerParams(vmem_limit_bytes=SMALL),
        cost_estimate=BRIEF,
        name="adjoint_blocks",
    )(which, slots, mine, other, goal, scale, *ahead)


def phase_steps():
    count, steps = lax.axis_size(PHASE), []
    while 2 ** len(steps) < count:
        steps.append(2 ** (len(steps) + 1) - 1)
    return steps


def combined(steps):
    masks = [0]
    for s in steps:
        masks += [m ^ s for m in masks]
    return masks


def sum_everywhere(x, axis, steps):
    for i, s in enumerate(steps):
        other = swap(x, axis, s).reshape(-1, 2, 2**i, *x.shape[1:])
        x = x + jnp.concatenate([other[:, 1:], other[:, :1]], axis=1).reshape(x.shape)
    return x


def gather_chips(by_phase):
    cores = core_count()
    by_chip = jnp.stack(spread(by_phase, VOX, range(cores, lax.axis_size(VOX), cores)))
    return spread(by_chip, VOX, range(1, cores))


def sum_chips(parts):
    cores = len(parts)
    chips = parts[0]
    for m in range(1, cores):
        chips = chips + swap(parts[m], VOX, m)
    mine = chips[0]
    for k in range(1, chips.shape[0]):
        mine = mine + swap(chips[k], VOX, k * cores)
    return mine


def cross(pieces):
    cores = len(pieces)
    crossed = [pieces[0]] + [swap(pieces[c], VOX, c) for c in range(1, cores)]
    return [jnp.stack([p[k] for p in crossed]) for k in range(pieces[0].shape[0])]


def send(chips):
    cores = core_count()
    return [chips[0]] + [swap(chips[k], VOX, k * cores) for k in range(1, len(chips))]


def exchange(pieces):
    return send(cross(pieces))


def hold_body(matrix, x, out):
    out[...] = x[0, :8, :]


def hold(matrix, x):
    return pl.pallas_call(
        hold_body,
        in_specs=specs(2, pltpu.VMEM),
        out_specs=pl.BlockSpec(memory_space=pltpu.VMEM),
        out_shape=jax.ShapeDtypeStruct((8, x.shape[-1]), F32),
        compiler_params=pltpu.CompilerParams(vmem_limit_bytes=LARGE),
        cost_estimate=BRIEF,
        name="hold",
    )(matrix, x)


def phase_stages(half):
    for step in phase_steps()[1:-1]:
        half = half + swap(half, PHASE, step)
    return half, swap(half, PHASE, phase_steps()[-1])


def tie(x, other):
    return lax.optimization_barrier((x, other))[0]


def goals_and_scales(structure, prescribed, importance, blocks, height):
    highest = lax.Precision.HIGHEST
    member = (structure[:, None] == jnp.arange(NSTRUCT, dtype=jnp.int32)[None, :]).astype(F32)
    target_dose = jnp.dot(member, prescribed, precision=highest, preferred_element_type=F32)
    voxel_weight = jnp.dot(
        member, importance[:, None], precision=highest, preferred_element_type=F32
    )
    voxel_weight = jnp.broadcast_to(voxel_weight, target_dose.shape)
    shape = (blocks, CHUNKS, height // CHUNKS, prescribed.shape[1])
    cut = [x.reshape(shape) for x in (target_dose, voxel_weight)]
    return [[x[:, h] for h in range(CHUNKS)] for x in cut]


def per_device(
    influence,
    weights,
    warp_tiles,
    owners,
    owner_slot,
    tile_index,
    structure,
    prescribed,
    importance,
    step_size,
):
    matrix = influence[0]
    vox_rows, spots = matrix.shape
    block_rows = warp_tiles.shape[1]
    rows, plans = weights.shape
    local_blocks = vox_rows // block_rows
    vox = lax.axis_size(VOX)
    phases = lax.axis_size(PHASE)
    cores = core_count()
    me_vox = lax.axis_index(VOX)
    me_phase = lax.axis_index(PHASE)
    slots_all = vox * CAP
    targets = owners[0, :, 0]
    which = ((me_phase ^ (me_phase >> 1)) & 1).astype(jnp.int32).reshape(1)

    def orders(names):
        before = jnp.tril(jnp.ones((local_blocks, local_blocks), jnp.int32), -1)
        same = (names[..., :, None] == names[..., None, :]).astype(jnp.int32)
        return jnp.sum(same * before, axis=-1)

    position = (targets ^ me_vox) * CAP + orders(targets)
    chosen_mask = jnp.arange(slots_all, dtype=jnp.int32)[:, None] == position[None, :]
    positions_i = jnp.arange(local_blocks, dtype=jnp.int32)
    source = jnp.sum(jnp.where(chosen_mask, positions_i[None, :], 0), axis=1)
    valid = jnp.sum(chosen_mask.astype(jnp.int32), axis=1)
    me = jnp.stack([me_vox, me_phase]).astype(jnp.int32)
    scalars = (source, valid, me)
    labels = jnp.zeros((LABEL_ROWS, plans), F32)
    labels = labels.at[0, :local_blocks].set(targets.astype(F32))
    labels = labels.at[1, :local_blocks].set(owner_slot[0].astype(F32))

    masks = combined(phase_steps())
    tiles = warp_tiles[tile_index[0]]
    held = jnp.concatenate(spread(weights, PHASE, masks[1:]), axis=0)
    for iteration in range(ITERS):
        last = iteration == ITERS - 1
        if iteration == 0:
            pieces = gather_chips(jnp.concatenate([held, labels], axis=0))
            infos = jnp.stack(pieces, axis=1).reshape(vox, -1, plans)[:, phases * rows :]
            names = infos[:, 0, :local_blocks].astype(jnp.int32)
            slots = infos[:, 1, :local_blocks].astype(jnp.int32)
            order = jnp.where(names == me_vox, orders(names), -1)
            hit = order[:, None, :] == jnp.arange(CAP, dtype=jnp.int32)[None, :, None]
            received = jnp.sum(jnp.where(hit, slots[:, None, :] + 1, 0), axis=-1)
            received = received.reshape(slots_all) - 1
        else:
            pieces = gather_chips(held)
        if rows % 16:
            every = jnp.stack(pieces, axis=1).reshape(vox, -1, plans)[:, : phases * rows]
            every = every.reshape(vox, phases, rows, plans)
            back_to = jnp.asarray([masks.index(p) for p in range(phases)], jnp.int32)
            every = every[jnp.arange(vox) ^ me_vox][:, back_to[jnp.arange(phases) ^ me_phase]]
            pieces = [every.transpose(1, 0, 2, 3).reshape(spots, plans)]
        ahead = [hold(matrix, held[None])] if iteration == 0 else []
        outgoing = forward(scalars, matrix, tiles, pieces, rows, vox, masks, ahead)
        returned, dose = [], []
        incoming, held_halves, seconds = exchange(outgoing[:cores]), [], []
        for h in range(CHUNKS):
            give, keep = place(which, received, incoming, local_blocks)
            got = swap(give, PHASE, 1)
            if iteration == 0 and h == 0:
                goals, scales = goals_and_scales(
                    tie(structure, give), prescribed, importance, local_blocks, block_rows
                )
            if h + 1 < CHUNKS:
                later = outgoing[(h + 1) * cores : (h + 2) * cores]
                incoming = exchange([tie(x, incoming[2]) for x in later])
            half, second = phase_stages(keep + got)
            held_halves.append(half)
            seconds.append(second)
        for h in range(CHUNKS):
            second = seconds[h] if h == 0 else tie(seconds[h], other)
            mine = held_halves[h] + second
            other = swap(mine, PHASE, 1)
            ahead = [hold(matrix, held_halves[1])] if iteration == 0 and h == 0 else []
            back = pull(which, received, mine, other, goals[h], scales[h], vox, last, ahead)
            returned += exchange(back[:cores])
            dose += back[cores:]
        parts = gradient_parts(scalars, matrix, tiles, returned, rows, vox, masks)
        if rows % 8:
            parts = parts[0].reshape(phases, vox, rows, plans)
            wanted = jnp.asarray(masks, jnp.int32) ^ me_phase
            parts = parts[wanted][:, jnp.arange(vox) ^ me_vox]
            parts = parts.transpose(1, 0, 2, 3).reshape(vox // cores, cores, phases * rows, plans)
            parts = [parts[:, c] for c in range(cores)]
        total = sum_chips(parts)
        if last:
            split = total.reshape(phases, rows, plans)
            total = split[0]
            for i, m in enumerate(masks[1:], 1):
                total = total + swap(split[i], PHASE, m)
            new_weights = jnp.maximum(held[:rows] - step_size[None, :] * total, 0.0)
        else:
            total = sum_everywhere(total.reshape(phases, rows, plans), PHASE, phase_steps())
            held = jnp.maximum(held - step_size[None, :] * total.reshape(held.shape), 0.0)
    dose_field = jnp.stack(dose, axis=1).reshape(vox_rows, plans)
    return (new_weights, dose_field)


def solution(mesh):
    in_specs = (
        P("phase", "vox", None),
        P(("phase", "vox"), None),
        P(),
        P("phase", "vox", None),
        P("phase", "vox"),
        P("phase", "vox"),
        P("vox"),
        P(),
        P(),
        P(),
    )
    out_specs = (P(("phase", "vox"), None), P("vox", None))
    return jax.shard_map(
        per_device, mesh=mesh, in_specs=in_specs, out_specs=out_specs, check_vma=False
    )
```
